256 devices in a mesh: dp: 8 (over y, core), ctx: 32 (over x, z).
Axes of the slice: x: 4, y: 4, z: 8, core: 2. Of those that a mesh axis runs over, the one named last changes fastest.
Arguments:
- queries: bfloat16 [131072, 256], P(('dp', 'ctx')), parts along dimension 0, may hold values from -90 to 90
- keys: bfloat16 [131072, 128], P(('dp', 'ctx')), parts along dimension 0, may hold values from -4.5 to 4.5
- values: bfloat16 [131072, 128], P(('dp', 'ctx')), parts along dimension 0, may hold values from -6 to 6
- cotangent: bfloat16 [131072, 256], P(('dp', 'ctx')), parts along dimension 0, may hold values from -6 to 6
- doc_lengths: int32 [512], P('dp'), parts along dimension 0, may hold values from 1 to 1024, 16384 in all
- old_slots: int32 [4096], P('dp'), parts along dimension 0, may hold values from 0 to 511, as said below
Outputs:
- attended: bfloat16 [131072, 256], P(('dp', 'ctx')), parts along dimension 0
- query_grad: float32 [131072, 256], P(('dp', 'ctx')), parts along dimension 0
- key_grad: float32 [131072, 128], P(('dp', 'ctx')), parts along dimension 0
- value_grad: float32 [131072, 128], P(('dp', 'ctx')), parts along dimension 0
The draws below stay inside these ranges and needn't reach their ends.
There are 8 independent parts, one for each index of `dp`. The reference program is written for one: setup_inputs(seed, part) draws one part's arguments, and reference() takes and returns one part's arrays. A program takes and returns all parts, laid end to end along the dimension named above; each array names one. Nothing has to cross between parts.
Inputs may be any that keep to these rules, and one draw needn't show every extreme that they name: `old_slots`: each old slot appears once. Old slot s lies on device s // 16 and block b on device b // 16. The 16 old slots of one device hold blocks of 16 different devices when 16 is at most the number of devices, else the same number of blocks of every device. `doc_lengths`: the lengths sum to 16384.
All inputs are finite; a program needn't handle non-finite values.
Results may differ from the reference program's by a relative error of at most 0.035.
Values may be sent and summed in bfloat16 or wider, within the bound.
A program may use at most 64 MiB of HBM per device.

```python
import math
import jax
import jax.numpy as jnp
import numpy as np
from jax import lax

HD = 128
QHEADS = 2
ROWS_DEV = 512
ROWS_BLK = 32
REACH = 2
SEQ = 16384
NBLK = 512
MAXDOC = 1024
NDOCS = 64
N_CTX = 32


def key_rows(key, share):
    base = jnp.clip(jax.random.normal(key, (SEQ, HD), jnp.float32), -4.0, 4.0)
    row_ids = jnp.arange(SEQ, dtype=jnp.int32)
    chosen = (jax.random.uniform(jax.random.fold_in(key, 11), (SEQ,)) < share) & (row_ids % 2 == 1)
    stretch = 1.0 + jax.random.uniform(jax.random.fold_in(key, 12), (SEQ, 1), minval=0.006, maxval=0.02)
    lifted = jnp.roll(base * stretch, -1, axis=0)
    chosen_next = jnp.roll(chosen, -1)
    return jnp.where(chosen_next[:, None], lifted, base)


def draw_keys(key, part):
    drawn = key_rows(key, 0.0)
    return drawn.astype(jnp.bfloat16)


def draw_queries(key, part):
    own_key = jax.random.fold_in(key, 5)
    noise = jnp.clip(jax.random.normal(own_key, (SEQ, QHEADS, HD), jnp.float32), -4.0, 4.0)
    return noise.reshape(SEQ, QHEADS * HD).astype(jnp.bfloat16)


def draw_old_slots(key, part):
    key = jax.random.fold_in(key, 21)
    members = N_CTX
    per_dev = ROWS_DEV // ROWS_BLK
    per_peer = max(1, per_dev // members)
    peers = per_dev // per_peer
    split_keys = jax.random.split(key, 4)
    outer = jax.random.permutation(split_keys[0], members).astype(jnp.int32)
    inner = jax.random.permutation(split_keys[1], members).astype(jnp.int32)
    offsets = jax.random.permutation(split_keys[2], members).astype(jnp.int32)[:peers]
    orders = jax.vmap(lambda sub: jax.random.permutation(sub, per_dev))(jax.random.split(split_keys[3], 2 * members)).astype(jnp.int32)
    dest_order = orders[:members]
    source_order = orders[members:]
    source = jnp.arange(members, dtype=jnp.int32)[:, None]
    offset_ids = jnp.arange(per_dev, dtype=jnp.int32)[None, :]
    target = outer[(inner[source] + offsets[offset_ids // per_peer]) % members]
    logical = target * per_dev + dest_order[target, offset_ids]
    slot = source * per_dev + source_order[source, offset_ids]
    return jnp.zeros((NBLK,), jnp.int32).at[logical.reshape(-1)].set(slot.reshape(-1))


def steps_of(rng, shape, pieces, low, top_value):
    level, own = 1.0, jax.random.fold_in(rng, 6)
    for position, blocks in pieces:
        heights = jnp.exp(jax.random.uniform(jax.random.fold_in(own, position), (blocks,), jnp.float32, low / len(pieces), top_value / len(pieces)))
        level = level * jnp.repeat(heights, shape[position] // blocks).reshape([-1 if axis == position else 1 for axis in range(len(shape))])
    return level


def length_profile(amount, total, limit, slope):
    loads = [(1 << 20) // math.isqrt(rank ** slope) + 1 for rank in range(2, amount + 1)]
    spare, counts = total - limit - (amount - 1), [1] * (amount - 1)
    while spare > 0:
        movable = [i for i in range(amount - 1) if counts[i] < limit]
        pool, remaining = sum([loads[i] for i in movable]), spare
        for i in movable:
            extra = min(limit - counts[i], max(1, remaining * loads[i] // pool), spare)
            counts[i] = counts[i] + extra
            spare = spare - extra
    return np.array([limit] + counts)


def uneven(rng, number_of, total, most, lean):
    if number_of == 2:
        one = jax.random.randint(rng, (), max(1, total - most), min(most, total - 1) + 1)
        return jnp.stack([one, total - one])
    tallies = jnp.asarray(length_profile(number_of, total, most, lean), jnp.int32)
    pairs = (number_of - 1) // 2
    giver, receiver = tallies[1:1 + 2 * pairs:2], tallies[2:2 + 2 * pairs:2]
    room = jnp.minimum(giver - 1, most - receiver)
    passed = jax.random.randint(jax.random.fold_in(rng, 1), (pairs,), 0, 1 << 20) % (room + 1)
    tallies = tallies.at[1:1 + 2 * pairs:2].set(giver - passed).at[2:2 + 2 * pairs:2].set(receiver + passed)
    return tallies[jax.random.permutation(jax.random.fold_in(rng, 2), number_of)]


def bell_draw(rng, shape, spread, limit, cuts=(), kind=jnp.bfloat16):
    entries = spread * jax.random.normal(rng, shape, jnp.float32)
    if cuts:
        entries = entries * steps_of(rng, shape, cuts, -0.22, 0.18)
    return jnp.clip(entries, -limit, limit).astype(kind)


def setup_inputs(seed: int = 0, part: int = 0) -> dict:
    key_of = jax.random.split(jax.random.key(seed), 7)
    own_keys = jax.random.split(jax.random.fold_in(key_of[6], part), 7)
    return {
        "queries": draw_queries(jax.random.fold_in(jax.random.fold_in(key_of[6], part), 71), part),
        "keys": draw_keys(jax.random.fold_in(jax.random.fold_in(key_of[6], part), 71), part),
        "values": bell_draw(own_keys[2], (SEQ, HD), 1.0, 6.0, ((0, 32),)),
        "cotangent": bell_draw(own_keys[3], (SEQ, QHEADS * HD), 1.0, 6.0, ((0, 32),)),
        "doc_lengths": uneven(own_keys[4], NDOCS, SEQ, MAXDOC, 2).astype(jnp.int32),
        "old_slots": draw_old_slots(jax.random.fold_in(jax.random.fold_in(key_of[6], part), 71), part),
    }


NEGATIVE = -1.0e30


def doc_index(positions, doc_ends):
    return jnp.sum((doc_ends[None, :] <= positions[:, None]).astype(jnp.int32), axis=1)


def reference(queries, keys, values, cotangent, doc_lengths, old_slots):
    def relay(array):
        blocks = array.reshape(NBLK, ROWS_BLK, array.shape[1])
        return jnp.take(blocks, old_slots, axis=0).reshape(array.shape)

    query_new = relay(queries)
    key_new = relay(keys)
    value_new = relay(values)
    doc_ends = jnp.cumsum(doc_lengths).astype(jnp.int32)
    factor = HD ** -0.5
    behind = REACH * ROWS_DEV
    span = behind + ROWS_DEV
    key_pad = jnp.concatenate([jnp.zeros((behind, HD), key_new.dtype), key_new], axis=0)
    value_pad = jnp.concatenate([jnp.zeros((behind, HD), value_new.dtype), value_new], axis=0)

    def step(carry, block_id):
        key_acc, value_acc = carry
        start = block_id * ROWS_DEV
        query_pos = start + jnp.arange(ROWS_DEV, dtype=jnp.int32)
        key_pos = start - behind + jnp.arange(span, dtype=jnp.int32)
        same_doc = doc_index(query_pos, doc_ends)[:, None] == doc_index(key_pos, doc_ends)[None, :]
        allowed = same_doc & (key_pos[None, :] <= query_pos[:, None]) & (key_pos[None, :] >= 0)
        query_block = lax.dynamic_slice_in_dim(query_new, start, ROWS_DEV, 0)
        grad_block = lax.dynamic_slice_in_dim(cotangent, start, ROWS_DEV, 0)
        key_window = lax.dynamic_slice_in_dim(key_pad, start, span, 0)
        value_window = lax.dynamic_slice_in_dim(value_pad, start, span, 0)
        out_list = []
        grad_list = []
        key_part = jnp.zeros((span, HD), jnp.float32)
        value_part = jnp.zeros((span, HD), jnp.float32)
        for head_id in range(QHEADS):
            query_head = query_block[:, head_id * HD:(head_id + 1) * HD]
            grad_head = grad_block[:, head_id * HD:(head_id + 1) * HD]
            raw = jnp.dot(query_head, key_window.T, preferred_element_type=jnp.float32) * factor
            scores = jnp.where(allowed, raw, NEGATIVE)
            peak = jnp.max(scores, axis=1)
            lse = peak + jnp.log(jnp.sum(jnp.exp(scores - peak[:, None]), axis=1))
            weights = jnp.exp(scores - lse[:, None])
            weights_low = weights.astype(jnp.bfloat16)
            out_head = jnp.dot(weights_low, value_window, preferred_element_type=jnp.float32).astype(jnp.bfloat16)
            delta = jnp.sum(grad_head.astype(jnp.float32) * out_head.astype(jnp.float32), axis=1)
            grad_weights = jnp.dot(grad_head, value_window.T, preferred_element_type=jnp.float32)
            grad_scores = (weights * (grad_weights - delta[:, None])).astype(jnp.bfloat16)
            grad_list.append(jnp.dot(grad_scores, key_window, preferred_element_type=jnp.float32) * factor)
            key_part = key_part + jnp.dot(grad_scores.T, query_head, preferred_element_type=jnp.float32)
            value_part = value_part + jnp.dot(weights_low.T, grad_head, preferred_element_type=jnp.float32)
            out_list.append(out_head)
        key_acc = lax.dynamic_update_slice_in_dim(key_acc, lax.dynamic_slice_in_dim(key_acc, start, span, 0) + key_part, start, 0)
        value_acc = lax.dynamic_update_slice_in_dim(value_acc, lax.dynamic_slice_in_dim(value_acc, start, span, 0) + value_part, start, 0)
        return (key_acc, value_acc), (jnp.concatenate(out_list, axis=1), jnp.concatenate(grad_list, axis=1))

    start_carry = (jnp.zeros((behind + SEQ, HD), jnp.float32), jnp.zeros((behind + SEQ, HD), jnp.float32))
    (key_acc, value_acc), (out_blocks, grad_blocks) = lax.scan(step, start_carry, jnp.arange(SEQ // ROWS_DEV, dtype=jnp.int32))
    attended = out_blocks.reshape(SEQ, QHEADS * HD)
    query_grad = grad_blocks.reshape(SEQ, QHEADS * HD)
    return attended, query_grad, key_acc[behind:] * factor, value_acc[behind:]
```

```python
import functools

import jax
import jax.numpy as jnp
from jax import lax
from jax.experimental import pallas as pl
from jax.experimental.pallas import tpu as pltpu
from jax.sharding import PartitionSpec as P

N = 32
NZ = 8
NX = 4
BLK = 32
PER = 16
ROWS = 512
HD = 128
WIN = 3 * ROWS
TILE = 256
NEGATIVE = -1e30
LOG2E = 1.4426950408889634
FACTOR = HD**-0.5
MESH = pl.DeviceIdType.MESH
BF = jnp.bfloat16
F32 = jnp.float32


def peer(index):
    return (lax.axis_index("dp"), index)


def near_first(count, step):
    return jnp.where(step % 2 == 1, (step + 1) // 2, (count - step // 2) % count)


def target_of(me, step):
    z = (me % NZ + near_first(NZ, step // NX)) % NZ
    x = (me // NZ + near_first(NX, step % NX)) % NX
    return x * NZ + z


def send(src, dst, send_sem, recv_sem, index):
    return pltpu.make_async_remote_copy(
        src, dst, send_sem, recv_sem, device_id=peer(index), device_id_type=MESH
    )


def gather_kernel(
    send_ids, recv_ids, q_ref, k_ref, v_ref, q_out, kv_out,
    kv_send, kv_recv, q_send, q_recv, window,
    kv_ssem, kv_rsem, q_ssem, q_rsem, h1_ssem, h1_rsem, h2_ssem, h2_rsem,
):
    me = lax.axis_index("ctx")
    right = (me + 1) % N
    barrier = pltpu.get_barrier_semaphore()

    def greet(step, carry):
        pl.semaphore_signal(
            barrier, inc=1, device_id=peer((me + step) % N), device_id_type=MESH
        )
        return carry

    lax.fori_loop(1, N, greet, 0)

    def pack(dest, carry):
        held = send_ids[dest]
        kv_send[dest, :, :HD] = k_ref[held]
        kv_send[dest, :, HD:] = v_ref[held]
        q_send[dest] = q_ref[held]
        return carry

    lax.fori_loop(0, N, pack, 0)
    kv_recv[me] = kv_send[me]
    q_recv[me] = q_send[me]
    pl.semaphore_wait(barrier, N - 1)

    def push_kv(step, carry):
        dest = target_of(me, step)
        send(kv_send.at[dest], kv_recv.at[me], kv_ssem, kv_rsem, dest).start()
        return carry

    def push_q(step, carry):
        dest = target_of(me, step)
        send(q_send.at[dest], q_recv.at[me], q_ssem, q_rsem, dest).start()
        return carry

    lax.fori_loop(1, N, push_kv, 0)
    lax.fori_loop(1, N, push_q, 0)

    def drain(buf, sem):
        part = buf.at[pl.ds(0, N - 1)]
        pltpu.make_async_copy(part, part, sem).wait()

    drain(kv_recv, kv_rsem)

    def unpack_kv(block, carry):
        window[pl.ds(pl.multiple_of(2 * ROWS + block * BLK, BLK), BLK)] = kv_recv[recv_ids[block]]
        return carry

    lax.fori_loop(0, PER, unpack_kv, 0)
    chunks = 4
    size = ROWS // chunks

    def hop(level, chunk, ssem, rsem):
        return send(
            window.at[pl.ds((2 - level) * ROWS + chunk * size, size)],
            window.at[pl.ds((1 - level) * ROWS + chunk * size, size)],
            ssem.at[chunk], rsem.at[chunk], right,
        )

    first = [hop(0, chunk, h1_ssem, h1_rsem) for chunk in range(chunks)]
    second = [hop(1, chunk, h2_ssem, h2_rsem) for chunk in range(chunks)]
    for copy in first:
        copy.start()
    for copy, onward in zip(first, second):
        copy.wait_recv()
        onward.start()
    drain(q_recv, q_rsem)

    def unpack_q(block, carry):
        q_out[pl.ds(pl.multiple_of(block * BLK, BLK), BLK)] = q_recv[recv_ids[block]]
        return carry

    lax.fori_loop(0, PER, unpack_q, 0)
    for copy in second:
        copy.wait_recv()
    kv_out[...] = window[...]
    for copy in first + second:
        copy.wait_send()
    drain(kv_send, kv_ssem)
    drain(q_send, q_ssem)


def compute_kernel(
    start_ref, q_ref, kv_ref, g_ref, att_ref, dq_ref, own_ref, mid_ref, far_ref,
    kt, vt, dkv,
):
    kt[...] = kv_ref[:, :HD].T
    vt[...] = kv_ref[:, HD:].T
    dkv[...] = jnp.zeros_like(dkv)
    span = 5 * TILE

    def step(index, carry):
        head, row = index // 2, index % 2
        rows = pl.ds(pl.multiple_of(row * TILE, TILE), TILE)
        cols = pl.ds(pl.multiple_of(head * HD, HD), HD)
        keys = pl.ds(pl.multiple_of(row * TILE, TILE), span)
        q = q_ref[rows, cols]
        g = g_ref[rows, cols]
        k = kv_ref[keys, :HD]
        v = kv_ref[keys, HD:]
        raw = lax.dot_general(k, q, (((1,), (1,)), ((), ())), preferred_element_type=F32)
        start = start_ref[:, rows] - row * TILE
        pos = lax.broadcasted_iota(jnp.int32, (span, TILE), 0)
        query = lax.broadcasted_iota(jnp.int32, (span, TILE), 1) + 4 * TILE
        scores = jnp.where((pos >= start) & (pos <= query), raw * (FACTOR * LOG2E), NEGATIVE)
        peak = jnp.max(scores, axis=0, keepdims=True)
        weights = jnp.exp2(scores - peak)
        total = jnp.sum(weights, axis=0, keepdims=True)
        weights = weights * (1.0 / total)
        low = weights.astype(BF)
        out = jnp.dot(vt[:, keys], low, preferred_element_type=F32).astype(BF)
        att_ref[rows, cols] = out.T
        gt = g.T.astype(F32)
        delta = jnp.sum(gt * out.astype(F32), axis=0, keepdims=True)
        dprobs = lax.dot_general(v, g, (((1,), (1,)), ((), ())), preferred_element_type=F32)
        dscores = (weights * (dprobs - delta)).astype(BF)
        dkv[keys, :HD] += jnp.dot(dscores, q, preferred_element_type=F32)
        dkv[keys, HD:] += jnp.dot(low, g, preferred_element_type=F32)
        dq = jnp.dot(kt[:, keys], dscores, preferred_element_type=F32) * FACTOR
        dq_ref[rows, cols] = dq.T
        return carry

    lax.fori_loop(0, 4, step, 0)
    dkv[:, :HD] = dkv[:, :HD] * FACTOR
    far_ref[...] = dkv[:ROWS].astype(BF)
    mid_ref[...] = dkv[ROWS : 2 * ROWS].astype(BF)
    own_ref[...] = dkv[2 * ROWS :]


def return_kernel(
    own_ref, mid_ref, far_ref, dk_ref, dv_ref, got_far, total, got_mid,
    s2_sem, r2_sem, s1_sem, r1_sem,
):
    me = lax.axis_index("ctx")
    left = (me + N - 1) % N
    right = (me + 1) % N
    barrier = pltpu.get_barrier_semaphore()
    for other in (left, right):
        pl.semaphore_signal(barrier, inc=1, device_id=peer(other), device_id_type=MESH)
    pl.semaphore_wait(barrier, 2)
    chunks = 4
    size = ROWS // chunks
    first = []
    second = []
    for chunk in range(chunks):
        part = pl.ds(chunk * size, size)
        first.append(send(far_ref.at[part], got_far.at[part], s2_sem.at[chunk], r2_sem.at[chunk], left))
        second.append(send(total.at[part], got_mid.at[part], s1_sem.at[chunk], r1_sem.at[chunk], left))
    for copy in first:
        copy.start()
    for chunk in range(chunks):
        part = pl.ds(chunk * size, size)
        first[chunk].wait_recv()
        total[part] = (mid_ref[part].astype(F32) + got_far[part].astype(F32)).astype(BF)
        second[chunk].start()
    for chunk in range(chunks):
        part = pl.ds(chunk * size, size)
        second[chunk].wait_recv()
        whole = own_ref[part] + got_mid[part].astype(F32)
        dk_ref[part] = whole[:, :HD]
        dv_ref[part] = whole[:, HD:]
    for copy in first + second:
        copy.wait_send()


def vmem(count):
    return [pl.BlockSpec(memory_space=pltpu.VMEM)] * count


def shape(*dims, dtype=BF):
    return jax.ShapeDtypeStruct(dims, dtype)


def on_device(queries, keys, values, cotangent, doc_lengths, old_slots):
    me = lax.axis_index("ctx")
    table = old_slots.reshape(N, PER)
    send_ids = jnp.sum(jnp.where(table // PER == me, table % PER, 0), axis=1)
    recv_ids = lax.dynamic_slice_in_dim(old_slots, me * PER, PER) // PER
    ends = jnp.cumsum(doc_lengths)
    starts = ends - doc_lengths
    pos = me * ROWS + jnp.arange(ROWS, dtype=jnp.int32)
    start = jnp.max(jnp.where(starts[:, None] <= pos[None, :], starts[:, None], 0), axis=0)
    start = (start - me * ROWS + 2 * ROWS).reshape(1, ROWS)

    smem = [pl.BlockSpec(memory_space=pltpu.SMEM)] * 2
    dma = pltpu.SemaphoreType.DMA
    buf = lambda *dims: pltpu.VMEM(dims, BF)
    q_new, kv = pl.pallas_call(
        gather_kernel,
        out_shape=[shape(ROWS, 2 * HD), shape(WIN, 2 * HD)],
        in_specs=smem + vmem(3),
        out_specs=vmem(2),
        scratch_shapes=[buf(N, BLK, 2 * HD)] * 4 + [buf(WIN, 2 * HD)]
        + [dma(())] * 4 + [dma((4,))] * 4,
        compiler_params=pltpu.CompilerParams(
            collective_id=0, has_side_effects=True, vmem_limit_bytes=32 << 20
        ),
        name="gather",
    )(
        send_ids, recv_ids,
        queries.reshape(PER, BLK, 2 * HD),
        keys.reshape(PER, BLK, HD),
        values.reshape(PER, BLK, HD),
    )
    attended, query_grad, own, mid, far = pl.pallas_call(
        compute_kernel,
        out_shape=[
            shape(ROWS, 2 * HD),
            shape(ROWS, 2 * HD, dtype=F32),
            shape(ROWS, 2 * HD, dtype=F32),
            shape(ROWS, 2 * HD),
            shape(ROWS, 2 * HD),
        ],
        in_specs=vmem(4),
        out_specs=vmem(5),
        scratch_shapes=[buf(HD, WIN), buf(HD, WIN), pltpu.VMEM((WIN, 2 * HD), F32)],
        compiler_params=pltpu.CompilerParams(vmem_limit_bytes=48 << 20),
        name="attend",
    )(start, q_new, kv, cotangent)
    key_grad, value_grad = pl.pallas_call(
        return_kernel,
        out_shape=[shape(ROWS, HD, dtype=F32)] * 2,
        in_specs=vmem(3),
        out_specs=vmem(2),
        scratch_shapes=[buf(ROWS, 2 * HD)] * 3 + [dma((4,))] * 4,
        compiler_params=pltpu.CompilerParams(
            collective_id=1, has_side_effects=True, vmem_limit_bytes=32 << 20
        ),
        name="give_back",
    )(own, mid, far)
    return attended, query_grad, key_grad, value_grad


def solution(mesh):
    rows = P(("dp", "ctx"), None)
    return jax.shard_map(
        on_device,
        mesh=mesh,
        in_specs=(rows, rows, rows, rows, P("dp"), P("dp")),
        out_specs=(rows, rows, rows, rows),
        check_vma=False,
    )
```

```python
import jax
import jax.numpy as jnp
from jax import lax
from jax.experimental import pallas as pl
from jax.experimental.pallas import tpu as pltpu
from jax.sharding import PartitionSpec as P

N = 32
NZ = 8
NX = 4
BLK = 32
PER = 16
ROWS = 512
HD = 128
HEADS = 2
WIN = 3 * ROWS
TILE = 256
COLS = HEADS * ROWS
NDOCS = 64
CHUNKS = 4
SIZE = ROWS // CHUNKS
NEGATIVE = -1e30
LOG2E = 1.4426950408889634
FACTOR = HD**-0.5
MESH = pl.DeviceIdType.MESH
BF = jnp.bfloat16
F32 = jnp.float32
BEHIND = (7, 6, 5)
AHEAD = (1, 2, 3)


def peer(index):
    return (lax.axis_index("dp"), index)


def send(src, dst, send_sem, recv_sem, index):
    return pltpu.make_async_remote_copy(
        src, dst, send_sem, recv_sem, device_id=peer(index), device_id_type=MESH
    )


def near_first(step):
    return jnp.where(step < 2, step, 5 - step)


def dot_nt(left, right):
    return lax.dot_general(left, right, (((1,), (1,)), ((), ())), preferred_element_type=F32)


def dot(left, right):
    return jnp.dot(left, right, preferred_element_type=F32)


class Exchange:
    def __init__(self, me, out, into, mid, out_sem, in_sem, mid_sem, onward_sem):
        self.me = me
        self.out, self.into, self.mid = out, into, mid
        self.out_sem, self.in_sem = out_sem, in_sem
        self.mid_sem, self.onward_sem = mid_sem, onward_sem

    def at(self, dx, dz):
        x = (self.me // NZ + dx) % NX
        z = (self.me % NZ + dz) % NZ
        return x * NZ + z

    def push(self, dz):
        def body(step, carry):
            dest = self.at(near_first(step), dz)
            send(self.out.at[dest], self.into.at[self.me], self.out_sem, self.in_sem, dest).start()
            return carry

        lax.fori_loop(1 if dz == 0 else 0, NX, body, 0)

    def push_far(self):
        def body(step, carry):
            dx = near_first(step)
            dest = self.at(dx, NZ // 2)
            way = self.at(dx, NZ - 2)
            send(self.out.at[dest], self.mid.at[step], self.out_sem, self.mid_sem, way).start()
            return carry

        lax.fori_loop(0, NX, body, 0)

    def pass_on(self):
        pltpu.make_async_copy(self.mid, self.mid, self.mid_sem).wait()
        dest = self.at(0, NZ - 2)

        def body(step, carry):
            source = self.at(NX - near_first(step), 2)
            send(self.mid.at[step], self.into.at[source], self.onward_sem, self.in_sem, dest).start()
            return carry

        lax.fori_loop(0, NX, body, 0)

    def received(self):
        part = self.into.at[pl.ds(0, N - 1)]
        pltpu.make_async_copy(part, part, self.in_sem).wait()

    def sent(self):
        part = self.out.at[pl.ds(0, N - 1)]
        pltpu.make_async_copy(part, part, self.out_sem).wait()
        pltpu.make_async_copy(self.mid, self.mid, self.onward_sem).wait()


def main_kernel(
    slots, lengths, q_hbm, k_hbm, v_hbm, g_hbm,
    att_ref, dq_ref, own_ref, got_mid,
    q_old, k_old, v_old, g_old, held_ids,
    kv_out, kv_into, kv_mid, q_out, q_into, q_mid,
    window, kt, vt, qs, gs, gt, starts,
    probs, dprobs, low, dscores, near_out, stats,
    far_out, got_far, mid_out,
    load_sem, kv_out_sem, kv_in_sem, kv_mid_sem, kv_on_sem, q_out_sem, q_in_sem, q_mid_sem, q_on_sem,
    h1_out, h1_in, h2_out, h2_in, f_out, f_in, m_out, m_in,
):
    me = lax.axis_index("ctx")
    left = (me + N - 1) % N
    right = (me + 1) % N
    loads = [
        pltpu.make_async_copy(src, dst, load_sem.at[i])
        for i, (src, dst) in enumerate(
            ((k_hbm, k_old), (v_hbm, v_old), (q_hbm, q_old), (g_hbm, g_old))
        )
    ]
    for load in loads:
        load.start()
    barrier = pltpu.get_barrier_semaphore()

    def greet(step, carry):
        pl.semaphore_signal(barrier, inc=1, device_id=peer((me + step) % N), device_id_type=MESH)
        return carry

    lax.fori_loop(1, N, greet, 0)

    def find(dest, carry):
        held = 0
        for j in range(PER):
            slot = slots[dest * PER + j]
            held = held + jnp.where(slot // PER == me, slot % PER, 0)
        held_ids[dest] = held
        return carry

    lax.fori_loop(0, N, find, 0)
    loads[0].wait()
    loads[1].wait()

    def pack_kv(dest, carry):
        held = held_ids[dest]
        kv_out[dest, :, :HD] = k_old[held]
        kv_out[dest, :, HD:] = v_old[held]
        return carry

    lax.fori_loop(0, N, pack_kv, 0)
    loads[2].wait()

    def pack_q(dest, carry):
        q_out[dest] = q_old[held_ids[dest]]
        return carry

    lax.fori_loop(0, N, pack_q, 0)
    kv_into[me] = kv_out[me]
    q_into[me] = q_out[me]
    pl.semaphore_wait(barrier, N - 1)

    kvs = Exchange(me, kv_out, kv_into, kv_mid, kv_out_sem, kv_in_sem, kv_mid_sem, kv_on_sem)
    queries = Exchange(me, q_out, q_into, q_mid, q_out_sem, q_in_sem, q_mid_sem, q_on_sem)
    kvs.push_far()
    kvs.push(0)
    for ahead, behind in zip(AHEAD, BEHIND):
        kvs.push(ahead)
        kvs.push(behind)
    kvs.pass_on()
    queries.push_far()
    queries.push(0)
    for behind in BEHIND:
        queries.push(behind)
    queries.pass_on()

    loads[3].wait()
    for half in range(2):
        for head in range(HEADS):
            cols = slice(half * ROWS + head * TILE, half * ROWS + (head + 1) * TILE)
            part = g_old[half * TILE : (half + 1) * TILE, head * HD : (head + 1) * HD]
            gs[cols] = part
            gt[:, cols] = part.T
    pos = lax.broadcasted_iota(jnp.int32, (1, ROWS), 1) + me * ROWS

    def find_start(doc, carry):
        begin, found = carry
        found = jnp.where(begin <= pos, begin, found)
        return begin + lengths[doc], found

    _, found = lax.fori_loop(0, NDOCS, find_start, (jnp.int32(0), jnp.zeros((1, ROWS), jnp.int32)))
    starts[...] = found - me * ROWS + 2 * ROWS

    kvs.received()

    def unpack_kv(block, carry):
        source = slots[me * PER + block] // PER
        window[pl.ds(pl.multiple_of(2 * ROWS + block * BLK, BLK), BLK)] = kv_into[source]
        return carry

    lax.fori_loop(0, PER, unpack_kv, 0)

    def hop(level, chunk, out_sem, in_sem):
        return send(
            window.at[pl.ds((2 - level) * ROWS + chunk * SIZE, SIZE)],
            window.at[pl.ds((1 - level) * ROWS + chunk * SIZE, SIZE)],
            out_sem.at[chunk], in_sem.at[chunk], right,
        )

    first = [hop(0, chunk, h1_out, h1_in) for chunk in range(CHUNKS)]
    second = [hop(1, chunk, h2_out, h2_in) for chunk in range(CHUNKS)]
    for copy in first:
        copy.start()
    for ahead in AHEAD:
        queries.push(ahead)
    for copy, onward in zip(first, second):
        copy.wait_recv()
        onward.start()
    kt[:, ROWS:] = window[ROWS:, :HD].T
    vt[:, ROWS:] = window[ROWS:, HD:].T

    def columns(half, head):
        return pl.ds(pl.multiple_of(half * ROWS + head * TILE, TILE), TILE)

    def near_rows(half):
        return slice(ROWS, 2 * ROWS + (half + 1) * TILE)

    def near_dprobs(half):
        rows = near_rows(half)

        def body(head, carry):
            cols = columns(half, head)
            dprobs[rows, cols] = dot_nt(window[rows, HD:], gs[cols])
            return carry

        lax.fori_loop(0, HEADS, body, 0)

    near_dprobs(0)
    near_dprobs(1)
    queries.received()

    def unpack_q(block, carry):
        source = slots[me * PER + block] // PER
        row = (block // 8) * ROWS + (block % 8) * BLK
        qs[pl.ds(pl.multiple_of(row, BLK), BLK)] = q_into[source, :, :HD]
        qs[pl.ds(pl.multiple_of(row + TILE, BLK), BLK)] = q_into[source, :, HD:]
        return carry

    lax.fori_loop(0, PER, unpack_q, 0)

    def near_forward(half):
        rows = near_rows(half)
        size = rows.stop - rows.start
        pos = lax.broadcasted_iota(jnp.int32, (size, TILE), 0) + ROWS
        query = lax.broadcasted_iota(jnp.int32, (size, TILE), 1) + (2 * ROWS + half * TILE)
        begin = starts[:, half * TILE : (half + 1) * TILE]

        def body(head, carry):
            cols = columns(half, head)
            raw = dot_nt(window[rows, :HD], qs[cols])
            scores = jnp.where((pos >= begin) & (pos <= query), raw * (FACTOR * LOG2E), NEGATIVE)
            peak = jnp.max(scores, axis=0, keepdims=True)
            weights = jnp.exp2(scores - peak)
            probs[rows, cols] = weights
            near_out[:, cols] = dot(vt[:, rows], weights.astype(BF))
            stats[0:1, cols] = peak
            stats[1:2, cols] = jnp.sum(weights, axis=0, keepdims=True)
            return carry

        lax.fori_loop(0, HEADS, body, 0)

    near_forward(0)
    near_forward(1)
    for copy in second:
        copy.wait_recv()
    kt[:, :ROWS] = window[:ROWS, :HD].T
    vt[:, :ROWS] = window[:ROWS, HD:].T

    def far_part(half):
        rows = slice(half * TILE, ROWS)
        size = rows.stop - rows.start
        pos = lax.broadcasted_iota(jnp.int32, (size, TILE), 0) + rows.start
        begin = starts[:, half * TILE : (half + 1) * TILE]

        def body(head, carry):
            cols = columns(half, head)
            raw = dot_nt(window[rows, :HD], qs[cols])
            scores = jnp.where(pos >= begin, raw * (FACTOR * LOG2E), NEGATIVE)
            near_peak = stats[0:1, cols]
            peak = jnp.maximum(near_peak, jnp.max(scores, axis=0, keepdims=True))
            rescale = jnp.exp2(near_peak - peak)
            weights = jnp.exp2(scores - peak)
            total = stats[1:2, cols] * rescale + jnp.sum(weights, axis=0, keepdims=True)
            inverse = 1.0 / total
            out = near_out[:, cols] * rescale + dot(vt[:, rows], weights.astype(BF))
            out = (out * inverse).astype(BF)
            att_ref[half * TILE : (half + 1) * TILE, pl.ds(pl.multiple_of(head * HD, HD), HD)] = out.T
            delta = jnp.sum(gt[:, cols].astype(F32) * out.astype(F32), axis=0, keepdims=True)
            weights = weights * inverse
            grad = dot_nt(window[rows, HD:], gs[cols])
            low[rows, cols] = weights.astype(BF)
            dscores[rows, cols] = (weights * (grad - delta)).astype(BF)
            stats[2:3, cols] = rescale * inverse
            stats[3:4, cols] = delta
            return carry

        lax.fori_loop(0, HEADS, body, 0)

    far_part(0)
    far_part(1)

    def key_sums(row, cols):
        rows = slice(row, row + SIZE)
        return dot(dscores[rows, cols], qs[cols]) * FACTOR, dot(low[rows, cols], gs[cols])

    back_far = []
    for chunk in range(CHUNKS):
        row = chunk * SIZE
        cols = slice(0, ROWS if row < TILE else COLS)
        dk, dv = key_sums(row, cols)
        part = slice(row, row + SIZE)
        far_out[part, :HD] = dk.astype(BF)
        far_out[part, HD:] = dv.astype(BF)
        copy = send(far_out.at[pl.ds(row, SIZE)], got_far.at[pl.ds(row, SIZE)], f_out.at[chunk], f_in.at[chunk], left)
        copy.start()
        back_far.append(copy)

    def near_back(half, rows):
        def body(head, carry):
            cols = columns(half, head)
            weights = probs[rows, cols] * stats[2:3, cols]
            low[rows, cols] = weights.astype(BF)
            dscores[rows, cols] = (weights * (dprobs[rows, cols] - stats[3:4, cols])).astype(BF)
            return carry

        lax.fori_loop(0, HEADS, body, 0)

    near_back(0, slice(ROWS, 2 * ROWS))
    near_back(1, slice(ROWS, 2 * ROWS))
    back_mid = []
    for chunk in range(CHUNKS):
        row = chunk * SIZE
        part = slice(row, row + SIZE)
        dk, dv = key_sums(ROWS + row, slice(0, COLS))
        back_far[chunk].wait_recv()
        mid_out[part, :HD] = (dk + got_far[part, :HD].astype(F32)).astype(BF)
        mid_out[part, HD:] = (dv + got_far[part, HD:].astype(F32)).astype(BF)
        copy = send(mid_out.at[pl.ds(row, SIZE)], got_mid.at[pl.ds(row, SIZE)], m_out.at[chunk], m_in.at[chunk], left)
        copy.start()
        back_mid.append(copy)

    near_back(0, slice(2 * ROWS, 2 * ROWS + TILE))
    near_back(1, slice(2 * ROWS, 3 * ROWS))
    for chunk in range(CHUNKS):
        row = chunk * SIZE
        part = slice(row, row + SIZE)
        cols = slice(0 if row < TILE else ROWS, COLS)
        dk, dv = key_sums(2 * ROWS + row, cols)
        own_ref[part, :HD] = dk
        own_ref[part, HD:] = dv

    def query_grad(half):
        rows = slice(half * TILE, 2 * ROWS + (half + 1) * TILE)

        def body(head, carry):
            cols = columns(half, head)
            grad = dot(kt[:, rows], dscores[rows, cols]) * FACTOR
            dq_ref[half * TILE : (half + 1) * TILE, pl.ds(pl.multiple_of(head * HD, HD), HD)] = grad.T
            return carry

        lax.fori_loop(0, HEADS, body, 0)

    query_grad(0)
    query_grad(1)
    kvs.sent()
    queries.sent()
    for copy in first + second + back_far + back_mid:
        copy.wait_send()
    for copy in back_mid:
        copy.wait_recv()


def finish_kernel(att, dq, own, got, att_ref, dq_ref, dk_ref, dv_ref, dk, dv, sems):
    copies = [
        pltpu.make_async_copy(src, dst, sems.at[i])
        for i, (src, dst) in enumerate(((att, att_ref), (dq, dq_ref), (dk, dk_ref), (dv, dv_ref)))
    ]
    copies[0].start()
    copies[1].start()
    dk[...] = own[:, :HD] + got[:, :HD].astype(F32)
    copies[2].start()
    dv[...] = own[:, HD:] + got[:, HD:].astype(F32)
    copies[3].start()
    for copy in copies:
        copy.wait()


def specs(space, count):
    return [pl.BlockSpec(memory_space=space)] * count


def shape(*dims, dtype=BF):
    return jax.ShapeDtypeStruct(dims, dtype)


def on_device(queries, keys, values, cotangent, doc_lengths, old_slots):
    dma = pltpu.SemaphoreType.DMA
    bf = lambda *dims: pltpu.VMEM(dims, BF)
    f32 = lambda *dims: pltpu.VMEM(dims, F32)
    slot_bufs = [bf(N, BLK, 2 * HD)] * 2 + [bf(NX, BLK, 2 * HD)]
    out_shape = [
        shape(ROWS, 2 * HD),
        shape(ROWS, 2 * HD, dtype=F32),
        shape(ROWS, 2 * HD, dtype=F32),
        shape(ROWS, 2 * HD),
    ]
    results = pl.pallas_call(
        main_kernel,
        out_shape=out_shape,
        in_specs=specs(pltpu.SMEM, 2) + specs(pltpu.HBM, 4),
        out_specs=specs(pltpu.VMEM, 4),
        scratch_shapes=[bf(PER, BLK, 2 * HD), bf(PER, BLK, HD), bf(PER, BLK, HD), bf(ROWS, 2 * HD)]
        + [pltpu.SMEM((N,), jnp.int32)]
        + slot_bufs * 2
        + [bf(WIN, 2 * HD), bf(HD, WIN), bf(HD, WIN), bf(COLS, HD), bf(COLS, HD), bf(HD, COLS)]
        + [pltpu.VMEM((1, ROWS), jnp.int32)]
        + [f32(WIN, COLS), f32(WIN, COLS), bf(WIN, COLS), bf(WIN, COLS), f32(HD, COLS), f32(8, COLS)]
        + [bf(ROWS, 2 * HD)] * 3
        + [dma((4,))]
        + [dma(())] * 8
        + [dma((CHUNKS,))] * 8,
        compiler_params=pltpu.CompilerParams(
            collective_id=0, has_side_effects=True, vmem_limit_bytes=48 << 20
        ),
        name="exchange_and_attend",
    )(
        old_slots, doc_lengths,
        queries.reshape(PER, BLK, 2 * HD),
        keys.reshape(PER, BLK, HD),
        values.reshape(PER, BLK, HD),
        cotangent,
    )
    return pl.pallas_call(
        finish_kernel,
        out_shape=out_shape[:2] + [shape(ROWS, HD, dtype=F32)] * 2,
        in_specs=specs(pltpu.VMEM, 4),
        out_specs=specs(pltpu.HBM, 4),
        scratch_shapes=[f32(ROWS, HD), f32(ROWS, HD), dma((4,))],
        compiler_params=pltpu.CompilerParams(vmem_limit_bytes=8 << 20),
        name="finish",
    )(*results)


def solution(mesh):
    rows = P(("dp", "ctx"), None)
    return jax.shard_map(
        on_device,
        mesh=mesh,
        in_specs=(rows, rows, rows, rows, P("dp"), P("dp")),
        out_specs=(rows, rows, rows, rows),
        check_vma=False,
    )
```

```python
import jax
import jax.numpy as jnp
from jax import lax
from jax.experimental import pallas as pl
from jax.experimental.pallas import tpu as pltpu
from jax.sharding import PartitionSpec as P

N = 32
NZ = 8
NX = 4
BLK = 32
PER = 16
ROWS = 512
HD = 128
HEADS = 2
WIN = 3 * ROWS
TILE = 256
COLS = HEADS * ROWS
NDOCS = 64
CHUNKS = 4
SIZE = ROWS // CHUNKS
NEGATIVE = -1e30
LOG2E = 1.4426950408889634
FACTOR = HD**-0.5
MESH = pl.DeviceIdType.MESH
BF = jnp.bfloat16
F32 = jnp.float32
BEHIND = (7, 6, 5)
AHEAD = (1, 2, 3)


def peer(index):
    return (lax.axis_index("dp"), index)


def send(src, dst, send_sem, recv_sem, index):
    return pltpu.make_async_remote_copy(
        src, dst, send_sem, recv_sem, device_id=peer(index), device_id_type=MESH
    )


def near_first(step):
    return jnp.where(step < 2, step, 5 - step)


def dot_nt(left, right):
    return lax.dot_general(left, right, (((1,), (1,)), ((), ())), preferred_element_type=F32)


def dot(left, right):
    return jnp.dot(left, right, preferred_element_type=F32)


class Exchange:
    def __init__(self, me, out, into, mid, out_sem, in_sem, mid_sem, onward_sem):
        self.me = me
        self.out, self.into, self.mid = out, into, mid
        self.out_sem, self.in_sem = out_sem, in_sem
        self.mid_sem, self.onward_sem = mid_sem, onward_sem

    def at(self, dx, dz):
        x = (self.me // NZ + dx) % NX
        z = (self.me % NZ + dz) % NZ
        return x * NZ + z

    def push(self, dz):
        def body(step, carry):
            dest = self.at(near_first(step), dz)
            send(self.out.at[dest], self.into.at[self.me], self.out_sem, self.in_sem, dest).start()
            return carry

        lax.fori_loop(1 if dz == 0 else 0, NX, body, 0)

    def push_far(self):
        def body(step, carry):
            dx = near_first(step)
            dest = self.at(dx, NZ // 2)
            way = self.at(dx, NZ - 2)
            send(self.out.at[dest], self.mid.at[step], self.out_sem, self.mid_sem, way).start()
            return carry

        lax.fori_loop(0, NX, body, 0)

    def pass_on(self):
        pltpu.make_async_copy(self.mid, self.mid, self.mid_sem).wait()
        dest = self.at(0, NZ - 2)

        def body(step, carry):
            source = self.at(NX - near_first(step), 2)
            send(self.mid.at[step], self.into.at[source], self.onward_sem, self.in_sem, dest).start()
            return carry

        lax.fori_loop(0, NX, body, 0)

    def received(self):
        part = self.into.at[pl.ds(0, N - 1)]
        pltpu.make_async_copy(part, part, self.in_sem).wait()

    def sent(self):
        part = self.out.at[pl.ds(0, N - 1)]
        pltpu.make_async_copy(part, part, self.out_sem).wait()

    def passed_on(self):
        pltpu.make_async_copy(self.mid, self.mid, self.onward_sem).wait()


def main_kernel(
    slots, lengths, q_hbm, k_hbm, v_hbm, g_hbm,
    att_hbm, dq_hbm, dk_hbm, dv_hbm,
    q_old, k_old, v_old, g_old, held_ids,
    kv_out, kv_into, kv_mid, q_out, q_into, q_mid,
    window, kt, vt, qs, gs, gt, starts,
    probs, dprobs, low, dscores, near_out, stats,
    far_out, got_far, mid_out, got_mid, att, dq, own, dk_all, dv_all,
    load_sem, store_sem, kv_out_sem, kv_in_sem, kv_mid_sem, kv_on_sem, q_out_sem, q_in_sem, q_mid_sem, q_on_sem,
    h1_out, h1_in, h2_out, h2_in, f_out, f_in, m_out, m_in,
):
    me = lax.axis_index("ctx")
    left = (me + N - 1) % N
    right = (me + 1) % N
    loads = [
        pltpu.make_async_copy(src, dst, load_sem.at[i])
        for i, (src, dst) in enumerate(
            ((k_hbm, k_old), (v_hbm, v_old), (q_hbm, q_old), (g_hbm, g_old))
        )
    ]
    for load in loads:
        load.start()
    barrier = pltpu.get_barrier_semaphore()

    def greet(step, carry):
        pl.semaphore_signal(barrier, inc=1, device_id=peer((me + step) % N), device_id_type=MESH)
        return carry

    lax.fori_loop(1, N, greet, 0)

    def find(dest, carry):
        held = 0
        for j in range(PER):
            slot = slots[dest * PER + j]
            held = held + jnp.where((slot >> 4) == me, slot & (PER - 1), 0)
        held_ids[dest] = held
        return carry

    lax.fori_loop(0, N, find, 0)
    loads[0].wait()
    loads[1].wait()

    def pack_kv(dest, carry):
        held = held_ids[dest]
        kv_out[dest, :, :HD] = k_old[held]
        kv_out[dest, :, HD:] = v_old[held]
        return carry

    lax.fori_loop(0, N, pack_kv, 0)
    kv_into[me] = kv_out[me]
    pl.semaphore_wait(barrier, N - 1)

    kvs = Exchange(me, kv_out, kv_into, kv_mid, kv_out_sem, kv_in_sem, kv_mid_sem, kv_on_sem)
    queries = Exchange(me, q_out, q_into, q_mid, q_out_sem, q_in_sem, q_mid_sem, q_on_sem)
    kvs.push(0)
    for ahead, behind in zip(AHEAD, BEHIND):
        kvs.push(ahead)
        kvs.push(behind)
    kvs.push(NZ // 2)

    loads[2].wait()

    def pack_q(dest, carry):
        q_out[dest] = q_old[held_ids[dest]]
        return carry

    lax.fori_loop(0, N, pack_q, 0)
    q_into[me] = q_out[me]
    queries.push_far()
    queries.push(0)
    for behind, ahead in zip(BEHIND, AHEAD):
        queries.push(behind)
        queries.push(ahead)

    loads[3].wait()
    for half in range(2):
        for head in range(HEADS):
            cols = slice(half * ROWS + head * TILE, half * ROWS + (head + 1) * TILE)
            part = g_old[half * TILE : (half + 1) * TILE, head * HD : (head + 1) * HD]
            gs[cols] = part
            gt[:, cols] = part.T
    pos = lax.broadcasted_iota(jnp.int32, (1, ROWS), 1) + me * ROWS

    def find_start(doc, carry):
        begin, found = carry
        found = jnp.where(begin <= pos, begin, found)
        return begin + lengths[doc], found

    _, found = lax.fori_loop(0, NDOCS, find_start, (jnp.int32(0), jnp.zeros((1, ROWS), jnp.int32)))
    starts[...] = found - me * ROWS + 2 * ROWS

    kvs.received()

    def unpack_kv(block, carry):
        source = slots[me * PER + block] >> 4
        window[pl.ds(pl.multiple_of(2 * ROWS + block * BLK, BLK), BLK)] = kv_into[source]
        return carry

    lax.fori_loop(0, PER, unpack_kv, 0)

    def hop(level, chunk, out_sem, in_sem):
        return send(
            window.at[pl.ds((2 - level) * ROWS + chunk * SIZE, SIZE)],
            window.at[pl.ds((1 - level) * ROWS + chunk * SIZE, SIZE)],
            out_sem.at[chunk], in_sem.at[chunk], right,
        )

    first = [hop(0, chunk, h1_out, h1_in) for chunk in range(CHUNKS)]
    second = [hop(1, chunk, h2_out, h2_in) for chunk in range(CHUNKS)]
    for copy in first:
        copy.start()
    queries.pass_on()
    for copy, onward in zip(first, second):
        copy.wait_recv()
        onward.start()
    kt[:, ROWS:] = window[ROWS:, :HD].T
    vt[:, ROWS:] = window[ROWS:, HD:].T

    def columns(half, head):
        return pl.ds(pl.multiple_of(half * ROWS + head * TILE, TILE), TILE)

    def near_rows(half):
        return slice(ROWS, 2 * ROWS + (half + 1) * TILE)

    def near_dprobs(half):
        rows = near_rows(half)

        def body(head, carry):
            cols = columns(half, head)
            dprobs[rows, cols] = dot_nt(window[rows, HD:], gs[cols])
            return carry

        lax.fori_loop(0, HEADS, body, 0)

    near_dprobs(0)
    near_dprobs(1)
    queries.received()

    def unpack_q(block, carry):
        source = slots[me * PER + block] >> 4
        row = (block // 8) * ROWS + (block % 8) * BLK
        qs[pl.ds(pl.multiple_of(row, BLK), BLK)] = q_into[source, :, :HD]
        qs[pl.ds(pl.multiple_of(row + TILE, BLK), BLK)] = q_into[source, :, HD:]
        return carry

    lax.fori_loop(0, PER, unpack_q, 0)

    def near_forward(half):
        rows = near_rows(half)
        size = rows.stop - rows.start
        pos = lax.broadcasted_iota(jnp.int32, (size, TILE), 0) + ROWS
        query = lax.broadcasted_iota(jnp.int32, (size, TILE), 1) + (2 * ROWS + half * TILE)
        begin = starts[:, half * TILE : (half + 1) * TILE]

        def body(head, carry):
            cols = columns(half, head)
            raw = dot_nt(window[rows, :HD], qs[cols])
            scores = jnp.where((pos >= begin) & (pos <= query), raw * (FACTOR * LOG2E), NEGATIVE)
            peak = jnp.max(scores, axis=0, keepdims=True)
            weights = jnp.exp2(scores - peak)
            probs[rows, cols] = weights
            near_out[:, cols] = dot(vt[:, rows], weights.astype(BF))
            stats[0:1, cols] = peak
            stats[1:2, cols] = jnp.sum(weights, axis=0, keepdims=True)
            return carry

        lax.fori_loop(0, HEADS, body, 0)

    near_forward(0)
    near_forward(1)

    def far_scores(half, row):
        rows = slice(row, row + SIZE)
        pos = lax.broadcasted_iota(jnp.int32, (SIZE, TILE), 0) + row
        begin = starts[:, half * TILE : (half + 1) * TILE]

        def body(head, carry):
            cols = columns(half, head)
            raw = dot_nt(window[rows, :HD], qs[cols])
            probs[rows, cols] = jnp.where(pos >= begin, raw * (FACTOR * LOG2E), NEGATIVE)
            dprobs[rows, cols] = dot_nt(window[rows, HD:], gs[cols])
            return carry

        lax.fori_loop(0, HEADS, body, 0)

    for chunk in range(CHUNKS):
        second[chunk].wait_recv()
        row = chunk * SIZE
        kt[:, row : row + SIZE] = window[row : row + SIZE, :HD].T
        vt[:, row : row + SIZE] = window[row : row + SIZE, HD:].T
        far_scores(0, row)
        if row >= TILE:
            far_scores(1, row)

    def far_part(half):
        rows = slice(half * TILE, ROWS)

        def body(head, carry):
            cols = columns(half, head)
            scores = probs[rows, cols]
            near_peak = stats[0:1, cols]
            peak = jnp.maximum(near_peak, jnp.max(scores, axis=0, keepdims=True))
            rescale = jnp.exp2(near_peak - peak)
            weights = jnp.exp2(scores - peak)
            total = stats[1:2, cols] * rescale + jnp.sum(weights, axis=0, keepdims=True)
            inverse = 1.0 / total
            out = near_out[:, cols] * rescale + dot(vt[:, rows], weights.astype(BF))
            out = (out * inverse).astype(BF)
            att[half * TILE : (half + 1) * TILE, pl.ds(pl.multiple_of(head * HD, HD), HD)] = out.T
            delta = jnp.sum(gt[:, cols].astype(F32) * out.astype(F32), axis=0, keepdims=True)
            weights = weights * inverse
            low[rows, cols] = weights.astype(BF)
            dscores[rows, cols] = (weights * (dprobs[rows, cols] - delta)).astype(BF)
            stats[2:3, cols] = rescale * inverse
            stats[3:4, cols] = delta
            return carry

        lax.fori_loop(0, HEADS, body, 0)

    far_part(0)
    far_part(1)

    def key_sums(row, cols):
        rows = slice(row, row + SIZE)
        return dot(dscores[rows, cols], qs[cols]) * FACTOR, dot(low[rows, cols], gs[cols])

    back_far = []
    for chunk in range(CHUNKS):
        row = chunk * SIZE
        cols = slice(0, ROWS if row < TILE else COLS)
        dk, dv = key_sums(row, cols)
        part = slice(row, row + SIZE)
        far_out[part, :HD] = dk.astype(BF)
        far_out[part, HD:] = dv.astype(BF)
        copy = send(far_out.at[pl.ds(row, SIZE)], got_far.at[pl.ds(row, SIZE)], f_out.at[chunk], f_in.at[chunk], left)
        copy.start()
        back_far.append(copy)

    def near_back(half, rows):
        def body(head, carry):
            cols = columns(half, head)
            weights = probs[rows, cols] * stats[2:3, cols]
            low[rows, cols] = weights.astype(BF)
            dscores[rows, cols] = (weights * (dprobs[rows, cols] - stats[3:4, cols])).astype(BF)
            return carry

        lax.fori_loop(0, HEADS, body, 0)

    near_back(0, slice(ROWS, 2 * ROWS))
    near_back(1, slice(ROWS, 2 * ROWS))
    back_mid = []
    for chunk in range(CHUNKS):
        row = chunk * SIZE
        part = slice(row, row + SIZE)
        dk, dv = key_sums(ROWS + row, slice(0, COLS))
        back_far[chunk].wait_recv()
        mid_out[part, :HD] = (dk + got_far[part, :HD].astype(F32)).astype(BF)
        mid_out[part, HD:] = (dv + got_far[part, HD:].astype(F32)).astype(BF)
        copy = send(mid_out.at[pl.ds(row, SIZE)], got_mid.at[pl.ds(row, SIZE)], m_out.at[chunk], m_in.at[chunk], left)
        copy.start()
        back_mid.append(copy)

    near_back(0, slice(2 * ROWS, 2 * ROWS + TILE))
    near_back(1, slice(2 * ROWS, 3 * ROWS))
    for chunk in range(CHUNKS):
        row = chunk * SIZE
        part = slice(row, row + SIZE)
        cols = slice(0 if row < TILE else ROWS, COLS)
        dk, dv = key_sums(2 * ROWS + row, cols)
        own[part, :HD] = dk
        own[part, HD:] = dv

    def query_grad(half):
        rows = slice(half * TILE, 2 * ROWS + (half + 1) * TILE)

        def body(head, carry):
            cols = columns(half, head)
            grad = dot(kt[:, rows], dscores[rows, cols]) * FACTOR
            dq[half * TILE : (half + 1) * TILE, pl.ds(pl.multiple_of(head * HD, HD), HD)] = grad.T
            return carry

        lax.fori_loop(0, HEADS, body, 0)

    query_grad(0)
    query_grad(1)
    stores = [
        pltpu.make_async_copy(src, dst, store_sem.at[i])
        for i, (src, dst) in enumerate(((att, att_hbm), (dq, dq_hbm)))
    ]
    for store in stores:
        store.start()
    for chunk in range(CHUNKS):
        rows = pl.ds(chunk * SIZE, SIZE)
        back_mid[chunk].wait_recv()
        dk_all[rows] = own[rows, :HD] + got_mid[rows, :HD].astype(F32)
        dv_all[rows] = own[rows, HD:] + got_mid[rows, HD:].astype(F32)
        for i, (src, dst) in enumerate(((dk_all, dk_hbm), (dv_all, dv_hbm))):
            store = pltpu.make_async_copy(src.at[rows], dst.at[rows], store_sem.at[2 + 2 * chunk + i])
            store.start()
            stores.append(store)
    kvs.sent()
    queries.sent()
    queries.passed_on()
    for copy in first + second + back_far + back_mid:
        copy.wait_send()
    for store in stores:
        store.wait()


def finish_kernel(*refs):
    results, places, held = refs[:4], refs[4:8], refs[8:12]
    load_sem, store_sem = refs[12:]
    loads = [pltpu.make_async_copy(results[i], held[i], load_sem.at[i]) for i in range(4)]
    stores = [pltpu.make_async_copy(held[i], places[i], store_sem.at[i]) for i in range(4)]
    for load in loads:
        load.start()
    for load, store in zip(loads, stores):
        load.wait()
        store.start()
    for store in stores:
        store.wait()


def specs(space, count):
    return [pl.BlockSpec(memory_space=space)] * count


def shape(*dims, dtype=BF):
    return jax.ShapeDtypeStruct(dims, dtype)


def on_device(queries, keys, values, cotangent, doc_lengths, old_slots):
    dma = pltpu.SemaphoreType.DMA
    bf = lambda *dims: pltpu.VMEM(dims, BF)
    f32 = lambda *dims: pltpu.VMEM(dims, F32)
    slot_bufs = [bf(N, BLK, 2 * HD)] * 2 + [bf(NX, BLK, 2 * HD)]
    out_shape = [
        shape(ROWS, 2 * HD),
        shape(ROWS, 2 * HD, dtype=F32),
        shape(ROWS, HD, dtype=F32),
        shape(ROWS, HD, dtype=F32),
    ]
    results = pl.pallas_call(
        main_kernel,
        out_shape=out_shape,
        in_specs=specs(pltpu.SMEM, 2) + specs(pltpu.HBM, 4),
        out_specs=specs(pltpu.HBM, 4),
        scratch_shapes=[bf(PER, BLK, 2 * HD), bf(PER, BLK, HD), bf(PER, BLK, HD), bf(ROWS, 2 * HD)]
        + [pltpu.SMEM((N,), jnp.int32)]
        + slot_bufs * 2
        + [bf(WIN, 2 * HD), bf(HD, WIN), bf(HD, WIN), bf(COLS, HD), bf(COLS, HD), bf(HD, COLS)]
        + [pltpu.VMEM((1, ROWS), jnp.int32)]
        + [f32(WIN, COLS), f32(WIN, COLS), bf(WIN, COLS), bf(WIN, COLS), f32(HD, COLS), f32(8, COLS)]
        + [bf(ROWS, 2 * HD)] * 5
        + [f32(ROWS, 2 * HD)] * 2
        + [f32(ROWS, HD)] * 2
        + [dma((4,)), dma((2 + 2 * CHUNKS,))]
        + [dma(())] * 8
        + [dma((CHUNKS,))] * 8,
        compiler_params=pltpu.CompilerParams(
            collective_id=0, has_side_effects=True, vmem_limit_bytes=56 << 20
        ),
        name="exchange_and_attend",
    )(
        old_slots, doc_lengths,
        queries.reshape(PER, BLK, 2 * HD),
        keys.reshape(PER, BLK, HD),
        values.reshape(PER, BLK, HD),
        cotangent,
    )
    return pl.pallas_call(
        finish_kernel,
        out_shape=out_shape,
        in_specs=specs(pltpu.HBM, 4),
        out_specs=specs(pltpu.HBM, 4),
        scratch_shapes=[bf(ROWS, 2 * HD), f32(ROWS, 2 * HD), f32(ROWS, HD), f32(ROWS, HD)]
        + [dma((4,))] * 2,
        compiler_params=pltpu.CompilerParams(vmem_limit_bytes=56 << 20),
        name="finish",
    )(*results)


def solution(mesh):
    rows = P(("dp", "ctx"), None)
    return jax.shard_map(
        on_device,
        mesh=mesh,
        in_specs=(rows, rows, rows, rows, P("dp"), P("dp")),
        out_specs=(rows, rows, rows, rows),
        check_vma=False,
    )
```

```python
import jax
import jax.numpy as jnp
from jax import lax
from jax.experimental import pallas as pl
from jax.experimental.pallas import tpu as pltpu
from jax.sharding import PartitionSpec as P

N = 32
NZ = 8
NX = 4
BLK = 32
PER = 16
ROWS = 512
HD = 128
HEADS = 2
WIN = 3 * ROWS
TILE = 256
COLS = HEADS * ROWS
NDOCS = 64
CHUNKS = 4
SIZE = ROWS // CHUNKS
NEGATIVE = -1e30
LOG2E = 1.4426950408889634
FACTOR = HD**-0.5
MESH = pl.DeviceIdType.MESH
BF = jnp.bfloat16
F32 = jnp.float32
BEHIND = (7, 6, 5)
AHEAD = (1, 2, 3)
ROUND = 1


def peer(index):
    return (lax.axis_index("dp"), index)


def send(src, dst, send_sem, recv_sem, index):
    return pltpu.make_async_remote_copy(
        src, dst, send_sem, recv_sem, device_id=peer(index), device_id_type=MESH
    )


def near_first(step):
    return jnp.where(step < 2, step, 5 - step)


def dot_nt(left, right):
    return lax.dot_general(left, right, (((1,), (1,)), ((), ())), preferred_element_type=F32)


def dot(left, right):
    return jnp.dot(left, right, preferred_element_type=F32)


class Exchange:
    def __init__(self, me, out, into, out_sem, in_sem, mid=None, mid_sem=None, onward_sem=None):
        self.me = me
        self.out, self.into, self.mid = out, into, mid
        self.out_sem, self.in_sem = out_sem, in_sem
        self.mid_sem, self.onward_sem = mid_sem, onward_sem

    def at(self, dx, dz):
        x = (self.me // NZ + dx) % NX
        z = (self.me % NZ + dz) % NZ
        return x * NZ + z

    def push(self, dz, first=0):
        def body(step, carry):
            dest = self.at(near_first(step), dz)
            send(self.out.at[dest], self.into.at[self.me], self.out_sem, self.in_sem, dest).start()
            return carry

        lax.fori_loop(first, NX, body, 0)

    def push_round(self, dz, spot, count):
        def body(step, carry):
            dx = near_first(step)
            dest = self.at(dx, dz)
            way = self.at(dx, NZ - 2)
            send(
                self.out.at[dest], self.mid.at[spot + step], self.out_sem, self.mid_sem, way
            ).start()
            return carry

        lax.fori_loop(0, count, body, 0)

    def mid_received(self):
        pltpu.make_async_copy(self.mid, self.mid, self.mid_sem).wait()

    def pass_on(self, dz, spot, count):
        dest = self.at(0, dz + 2)

        def body(step, carry):
            source = self.at(NX - near_first(step), 2)
            send(
                self.mid.at[spot + step], self.into.at[source], self.onward_sem, self.in_sem, dest
            ).start()
            return carry

        lax.fori_loop(0, count, body, 0)

    def received(self):
        part = self.into.at[pl.ds(0, N - 1)]
        pltpu.make_async_copy(part, part, self.in_sem).wait()

    def sent(self):
        part = self.out.at[pl.ds(0, N - 1)]
        pltpu.make_async_copy(part, part, self.out_sem).wait()

    def passed_on(self):
        pltpu.make_async_copy(self.mid, self.mid, self.onward_sem).wait()


def main_kernel(
    slots, lengths, q_hbm, k_hbm, v_hbm, g_hbm,
    att_hbm, dq_hbm, dk_hbm, dv_hbm,
    q_old, k_old, v_old, g_old, held_ids,
    kv_out, kv_into, q_out, q_into, q_mid,
    window, kt, vt, qs, gs, gt, starts,
    probs, dprobs, low, dscores, near_out, stats,
    far_out, got_far, mid_out, got_mid, att, dq, own, dk_all, dv_all,
    load_sem, store_sem, kv_out_sem, kv_in_sem, q_out_sem, q_in_sem, q_mid_sem, q_on_sem,
    h1_out, h1_in, h2_out, h2_in, f_out, f_in, m_out, m_in,
):
    me = lax.axis_index("ctx")
    left = (me + N - 1) % N
    right = (me + 1) % N
    loads = [
        pltpu.make_async_copy(src, dst, load_sem.at[i])
        for i, (src, dst) in enumerate(
            ((k_hbm, k_old), (v_hbm, v_old), (q_hbm, q_old), (g_hbm, g_old))
        )
    ]
    for load in loads:
        load.start()
    barrier = pltpu.get_barrier_semaphore()

    def greet(step, carry):
        pl.semaphore_signal(barrier, inc=1, device_id=peer((me + step) % N), device_id_type=MESH)
        return carry

    lax.fori_loop(1, N, greet, 0)

    def find(dest, carry):
        held = 0
        for j in range(PER):
            slot = slots[dest * PER + j]
            held = held + jnp.where((slot >> 4) == me, slot & (PER - 1), 0)
        held_ids[dest] = held
        return carry

    lax.fori_loop(0, N, find, 0)
    loads[0].wait()
    loads[1].wait()

    def pack_kv(dest, carry):
        held = held_ids[dest]
        kv_out[dest, :, :HD] = k_old[held]
        kv_out[dest, :, HD:] = v_old[held]
        return carry

    lax.fori_loop(0, N, pack_kv, 0)
    kv_into[me] = kv_out[me]
    pl.semaphore_wait(barrier, N - 1)

    kvs = Exchange(me, kv_out, kv_into, kv_out_sem, kv_in_sem)
    queries = Exchange(me, q_out, q_into, q_out_sem, q_in_sem, q_mid, q_mid_sem, q_on_sem)
    kvs.push(0, 1)
    for ahead, behind in zip(AHEAD, BEHIND):
        kvs.push(ahead)
        kvs.push(behind)
    kvs.push(NZ // 2)

    loads[2].wait()

    def pack_q(dest, carry):
        q_out[dest] = q_old[held_ids[dest]]
        return carry

    lax.fori_loop(0, N, pack_q, 0)
    q_into[me] = q_out[me]
    queries.push_round(NZ // 2, 0, NX)
    queries.push_round(AHEAD[-1], NX, ROUND)
    queries.push(0, 1)
    for behind, ahead in zip(BEHIND, AHEAD):
        queries.push(behind)
        queries.push(ahead, ROUND if ahead == AHEAD[-1] else 0)

    loads[3].wait()
    for half in range(2):
        for head in range(HEADS):
            cols = slice(half * ROWS + head * TILE, half * ROWS + (head + 1) * TILE)
            part = g_old[half * TILE : (half + 1) * TILE, head * HD : (head + 1) * HD]
            gs[cols] = part
            gt[:, cols] = part.T
    pos = lax.broadcasted_iota(jnp.int32, (1, ROWS), 1) + me * ROWS

    def find_start(doc, carry):
        begin, found = carry
        found = jnp.where(begin <= pos, begin, found)
        return begin + lengths[doc], found

    _, found = lax.fori_loop(0, NDOCS, find_start, (jnp.int32(0), jnp.zeros((1, ROWS), jnp.int32)))
    starts[...] = found - me * ROWS + 2 * ROWS

    kvs.received()

    def unpack_kv(block, carry):
        source = slots[me * PER + block] >> 4
        window[pl.ds(pl.multiple_of(2 * ROWS + block * BLK, BLK), BLK)] = kv_into[source]
        return carry

    lax.fori_loop(0, PER, unpack_kv, 0)

    def hop(level, chunk, out_sem, in_sem):
        return send(
            window.at[pl.ds((2 - level) * ROWS + chunk * SIZE, SIZE)],
            window.at[pl.ds((1 - level) * ROWS + chunk * SIZE, SIZE)],
            out_sem.at[chunk], in_sem.at[chunk], right,
        )

    first = [hop(0, chunk, h1_out, h1_in) for chunk in range(CHUNKS)]
    second = [hop(1, chunk, h2_out, h2_in) for chunk in range(CHUNKS)]
    for copy in first:
        copy.start()
    queries.mid_received()
    queries.pass_on(NZ // 2, 0, NX)
    queries.pass_on(AHEAD[-1], NX, ROUND)
    for copy, onward in zip(first, second):
        copy.wait_recv()
        onward.start()
    kt[:, ROWS:] = window[ROWS:, :HD].T
    vt[:, ROWS:] = window[ROWS:, HD:].T

    def columns(half, head):
        return pl.ds(pl.multiple_of(half * ROWS + head * TILE, TILE), TILE)

    def near_rows(half):
        return slice(ROWS, 2 * ROWS + (half + 1) * TILE)

    def near_dprobs(half):
        rows = near_rows(half)

        def body(head, carry):
            cols = columns(half, head)
            dprobs[rows, cols] = dot_nt(window[rows, HD:], gs[cols])
            return carry

        lax.fori_loop(0, HEADS, body, 0, unroll=True)

    near_dprobs(0)
    near_dprobs(1)
    queries.received()

    def unpack_q(block, carry):
        source = slots[me * PER + block] >> 4
        row = (block // 8) * ROWS + (block % 8) * BLK
        qs[pl.ds(pl.multiple_of(row, BLK), BLK)] = q_into[source, :, :HD]
        qs[pl.ds(pl.multiple_of(row + TILE, BLK), BLK)] = q_into[source, :, HD:]
        return carry

    lax.fori_loop(0, PER, unpack_q, 0)

    def near_forward(half):
        rows = near_rows(half)
        size = rows.stop - rows.start
        pos = lax.broadcasted_iota(jnp.int32, (size, TILE), 0) + ROWS
        query = lax.broadcasted_iota(jnp.int32, (size, TILE), 1) + (2 * ROWS + half * TILE)
        begin = starts[:, half * TILE : (half + 1) * TILE]

        def body(head, carry):
            cols = columns(half, head)
            raw = dot_nt(window[rows, :HD], qs[cols])
            scores = jnp.where((pos >= begin) & (pos <= query), raw * (FACTOR * LOG2E), NEGATIVE)
            peak = jnp.max(scores, axis=0, keepdims=True)
            weights = jnp.exp2(scores - peak)
            probs[rows, cols] = weights
            near_out[:, cols] = dot(vt[:, rows], weights.astype(BF))
            stats[0:1, cols] = peak
            stats[1:2, cols] = jnp.sum(weights, axis=0, keepdims=True)
            return carry

        lax.fori_loop(0, HEADS, body, 0, unroll=True)

    near_forward(0)
    near_forward(1)

    def far_scores(half, row):
        rows = slice(row, row + SIZE)
        pos = lax.broadcasted_iota(jnp.int32, (SIZE, TILE), 0) + row
        begin = starts[:, half * TILE : (half + 1) * TILE]

        def body(head, carry):
            cols = columns(half, head)
            raw = dot_nt(window[rows, :HD], qs[cols])
            probs[rows, cols] = jnp.where(pos >= begin, raw * (FACTOR * LOG2E), NEGATIVE)
            dprobs[rows, cols] = dot_nt(window[rows, HD:], gs[cols])
            return carry

        lax.fori_loop(0, HEADS, body, 0, unroll=True)

    for chunk in range(CHUNKS):
        second[chunk].wait_recv()
        row = chunk * SIZE
        vt[:, row : row + SIZE] = window[row : row + SIZE, HD:].T
        far_scores(0, row)
        if row >= TILE:
            far_scores(1, row)

    def far_part(half):
        rows = slice(half * TILE, ROWS)

        def body(head, carry):
            cols = columns(half, head)
            scores = probs[rows, cols]
            near_peak = stats[0:1, cols]
            peak = jnp.maximum(near_peak, jnp.max(scores, axis=0, keepdims=True))
            rescale = jnp.exp2(near_peak - peak)
            weights = jnp.exp2(scores - peak)
            total = stats[1:2, cols] * rescale + jnp.sum(weights, axis=0, keepdims=True)
            inverse = 1.0 / total
            out = near_out[:, cols] * rescale + dot(vt[:, rows], weights.astype(BF))
            out = (out * inverse).astype(BF)
            att[half * TILE : (half + 1) * TILE, pl.ds(pl.multiple_of(head * HD, HD), HD)] = out.T
            delta = jnp.sum(gt[:, cols].astype(F32) * out.astype(F32), axis=0, keepdims=True)
            weights = weights * inverse
            low[rows, cols] = weights.astype(BF)
            dscores[rows, cols] = (weights * (dprobs[rows, cols] - delta)).astype(BF)
            stats[2:3, cols] = rescale * inverse
            stats[3:4, cols] = delta
            return carry

        lax.fori_loop(0, HEADS, body, 0, unroll=True)

    def key_sums(row, cols):
        rows = slice(row, row + SIZE)
        return dot(dscores[rows, cols], qs[cols]) * FACTOR, dot(low[rows, cols], gs[cols])

    back_far = []
    for chunk in range(CHUNKS):
        row = chunk * SIZE
        if row == 0:
            far_part(0)
        if row == TILE:
            far_part(1)
        cols = slice(0, ROWS if row < TILE else COLS)
        dk, dv = key_sums(row, cols)
        part = slice(row, row + SIZE)
        far_out[part, :HD] = dk.astype(BF)
        far_out[part, HD:] = dv.astype(BF)
        copy = send(far_out.at[pl.ds(row, SIZE)], got_far.at[pl.ds(row, SIZE)], f_out.at[chunk], f_in.at[chunk], left)
        copy.start()
        back_far.append(copy)

    kt[:, :ROWS] = window[:ROWS, :HD].T

    def near_back(half, rows):
        def body(head, carry):
            cols = columns(half, head)
            weights = probs[rows, cols] * stats[2:3, cols]
            low[rows, cols] = weights.astype(BF)
            dscores[rows, cols] = (weights * (dprobs[rows, cols] - stats[3:4, cols])).astype(BF)
            return carry

        lax.fori_loop(0, HEADS, body, 0, unroll=True)

    near_back(0, slice(ROWS, 2 * ROWS))
    near_back(1, slice(ROWS, 2 * ROWS))
    back_mid = []
    for chunk in range(CHUNKS):
        row = chunk * SIZE
        part = slice(row, row + SIZE)
        dk, dv = key_sums(ROWS + row, slice(0, COLS))
        back_far[chunk].wait_recv()
        mid_out[part, :HD] = (dk + got_far[part, :HD].astype(F32)).astype(BF)
        mid_out[part, HD:] = (dv + got_far[part, HD:].astype(F32)).astype(BF)
        copy = send(mid_out.at[pl.ds(row, SIZE)], got_mid.at[pl.ds(row, SIZE)], m_out.at[chunk], m_in.at[chunk], left)
        copy.start()
        back_mid.append(copy)

    near_back(0, slice(2 * ROWS, 2 * ROWS + TILE))
    near_back(1, slice(2 * ROWS, 3 * ROWS))
    for chunk in range(CHUNKS):
        row = chunk * SIZE
        part = slice(row, row + SIZE)
        cols = slice(0 if row < TILE else ROWS, COLS)
        dk, dv = key_sums(2 * ROWS + row, cols)
        own[part, :HD] = dk
        own[part, HD:] = dv

    def query_grad(half):
        rows = slice(half * TILE, 2 * ROWS + (half + 1) * TILE)

        def body(head, carry):
            cols = columns(half, head)
            grad = dot(kt[:, rows], dscores[rows, cols]) * FACTOR
            dq[half * TILE : (half + 1) * TILE, pl.ds(pl.multiple_of(head * HD, HD), HD)] = grad.T
            return carry

        lax.fori_loop(0, HEADS, body, 0, unroll=True)

    query_grad(0)
    query_grad(1)
    stores = [
        pltpu.make_async_copy(src, dst, store_sem.at[i])
        for i, (src, dst) in enumerate(((att, att_hbm), (dq, dq_hbm)))
    ]
    for store in stores:
        store.start()
    for chunk in range(CHUNKS):
        rows = pl.ds(chunk * SIZE, SIZE)
        back_mid[chunk].wait_recv()
        dk_all[rows] = own[rows, :HD] + got_mid[rows, :HD].astype(F32)
        dv_all[rows] = own[rows, HD:] + got_mid[rows, HD:].astype(F32)
        for i, (src, dst) in enumerate(((dk_all, dk_hbm), (dv_all, dv_hbm))):
            store = pltpu.make_async_copy(src.at[rows], dst.at[rows], store_sem.at[2 + 2 * chunk + i])
            store.start()
            stores.append(store)
    kvs.sent()
    queries.sent()
    queries.passed_on()
    for copy in first + second + back_far + back_mid:
        copy.wait_send()
    for store in stores:
        store.wait()


def finish_kernel(*refs):
    results, places, held = refs[:4], refs[4:8], refs[8:12]
    load_sem, store_sem = refs[12:]
    loads = [pltpu.make_async_copy(results[i], held[i], load_sem.at[i]) for i in range(4)]
    stores = [pltpu.make_async_copy(held[i], places[i], store_sem.at[i]) for i in range(4)]
    for load in loads:
        load.start()
    for load, store in zip(loads, stores):
        load.wait()
        store.start()
    for store in stores:
        store.wait()


def specs(space, count):
    return [pl.BlockSpec(memory_space=space)] * count


def shape(*dims, dtype=BF):
    return jax.ShapeDtypeStruct(dims, dtype)


def on_device(queries, keys, values, cotangent, doc_lengths, old_slots):
    dma = pltpu.SemaphoreType.DMA
    bf = lambda *dims: pltpu.VMEM(dims, BF)
    f32 = lambda *dims: pltpu.VMEM(dims, F32)
    out_shape = [
        shape(ROWS, 2 * HD),
        shape(ROWS, 2 * HD, dtype=F32),
        shape(ROWS, HD, dtype=F32),
        shape(ROWS, HD, dtype=F32),
    ]
    results = pl.pallas_call(
        main_kernel,
        out_shape=out_shape,
        in_specs=specs(pltpu.SMEM, 2) + specs(pltpu.HBM, 4),
        out_specs=specs(pltpu.HBM, 4),
        scratch_shapes=[bf(PER, BLK, 2 * HD), bf(PER, BLK, HD), bf(PER, BLK, HD), bf(ROWS, 2 * HD)]
        + [pltpu.SMEM((N,), jnp.int32)]
        + [bf(N, BLK, 2 * HD)] * 4
        + [bf(NX + ROUND, BLK, 2 * HD)]
        + [bf(WIN, 2 * HD), bf(HD, WIN), bf(HD, WIN), bf(COLS, HD), bf(COLS, HD), bf(HD, COLS)]
        + [pltpu.VMEM((1, ROWS), jnp.int32)]
        + [f32(WIN, COLS), f32(WIN, COLS), bf(WIN, COLS), bf(WIN, COLS), f32(HD, COLS), f32(8, COLS)]
        + [bf(ROWS, 2 * HD)] * 5
        + [f32(ROWS, 2 * HD)] * 2
        + [f32(ROWS, HD)] * 2
        + [dma((4,)), dma((2 + 2 * CHUNKS,))]
        + [dma(())] * 6
        + [dma((CHUNKS,))] * 8,
        compiler_params=pltpu.CompilerParams(
            collective_id=0, has_side_effects=True, vmem_limit_bytes=56 << 20
        ),
        name="exchange_and_attend",
    )(
        old_slots, doc_lengths,
        queries.reshape(PER, BLK, 2 * HD),
        keys.reshape(PER, BLK, HD),
        values.reshape(PER, BLK, HD),
        cotangent,
    )
    return pl.pallas_call(
        finish_kernel,
        out_shape=out_shape,
        in_specs=specs(pltpu.HBM, 4),
        out_specs=specs(pltpu.HBM, 4),
        scratch_shapes=[bf(ROWS, 2 * HD), f32(ROWS, 2 * HD), f32(ROWS, HD), f32(ROWS, HD)]
        + [dma((4,))] * 2,
        compiler_params=pltpu.CompilerParams(vmem_limit_bytes=56 << 20),
        name="finish",
    )(*results)


def solution(mesh):
    rows = P(("dp", "ctx"), None)
    return jax.shard_map(
        on_device,
        mesh=mesh,
        in_specs=(rows, rows, rows, rows, P("dp"), P("dp")),
        out_specs=(rows, rows, rows, rows),
        check_vma=False,
    )
```

```python
import jax
import jax.numpy as jnp
from jax import lax
from jax.experimental import pallas as pl
from jax.experimental.pallas import tpu as pltpu
from jax.sharding import PartitionSpec as P

N = 32
NZ = 8
NX = 4
BLK = 32
PER = 16
ROWS = 512
HD = 128
HEADS = 2
WIN = 3 * ROWS
TILE = 256
COLS = HEADS * ROWS
NDOCS = 64
CHUNKS = 4
SIZE = ROWS // CHUNKS
NEGATIVE = -1e30
LOG2E = 1.4426950408889634
FACTOR = HD**-0.5
MESH = pl.DeviceIdType.MESH
BF = jnp.bfloat16
F32 = jnp.float32
BEHIND = (7, 6, 5)
AHEAD = (1, 2, 3)
ROUND = 1


def peer(index):
    return (lax.axis_index("dp"), index)


def send(src, dst, send_sem, recv_sem, index):
    return pltpu.make_async_remote_copy(
        src, dst, send_sem, recv_sem, device_id=peer(index), device_id_type=MESH
    )


def near_first(step):
    return jnp.where(step < 2, step, 5 - step)


def dot_nt(left, right):
    return lax.dot_general(left, right, (((1,), (1,)), ((), ())), preferred_element_type=F32)


def dot(left, right):
    return jnp.dot(left, right, preferred_element_type=F32)


class Exchange:
    def __init__(self, me, out, into, out_sem, in_sem, mid=None, mid_sem=None, onward_sem=None):
        self.me = me
        self.out, self.into, self.mid = out, into, mid
        self.out_sem, self.in_sem = out_sem, in_sem
        self.mid_sem, self.onward_sem = mid_sem, onward_sem

    def at(self, dx, dz):
        x = (self.me // NZ + dx) % NX
        z = (self.me % NZ + dz) % NZ
        return x * NZ + z

    def push(self, dz, first=0):
        def body(step, carry):
            dest = self.at(near_first(step), dz)
            send(self.out.at[dest], self.into.at[self.me], self.out_sem, self.in_sem, dest).start()
            return carry

        lax.fori_loop(first, NX, body, 0)

    def push_round(self, dz, spot, count):
        def body(step, carry):
            dx = near_first(step)
            dest = self.at(dx, dz)
            way = self.at(dx, NZ - 2)
            send(
                self.out.at[dest], self.mid.at[spot + step], self.out_sem, self.mid_sem, way
            ).start()
            return carry

        lax.fori_loop(0, count, body, 0)

    def mid_received(self):
        pltpu.make_async_copy(self.mid, self.mid, self.mid_sem).wait()

    def pass_on(self, dz, spot, count):
        dest = self.at(0, dz + 2)

        def body(step, carry):
            source = self.at(NX - near_first(step), 2)
            send(
                self.mid.at[spot + step], self.into.at[source], self.onward_sem, self.in_sem, dest
            ).start()
            return carry

        lax.fori_loop(0, count, body, 0)

    def received(self):
        part = self.into.at[pl.ds(0, N - 1)]
        pltpu.make_async_copy(part, part, self.in_sem).wait()

    def sent(self):
        part = self.out.at[pl.ds(0, N - 1)]
        pltpu.make_async_copy(part, part, self.out_sem).wait()

    def passed_on(self):
        pltpu.make_async_copy(self.mid, self.mid, self.onward_sem).wait()


def main_kernel(
    slots, lengths, q_hbm, k_hbm, v_hbm, g_hbm,
    att_hbm, dq_hbm, own_hbm, got_hbm,
    q_old, k_old, v_old, g_old, held_ids,
    kv_out, kv_into, q_out, q_into, q_mid,
    window, kt, vt, qs, gs, gt, starts,
    probs, dprobs, low, dscores, near_out, stats,
    far_out, got_far, mid_out, att, dq, own,
    load_sem, store_sem, kv_out_sem, kv_in_sem, q_out_sem, q_in_sem, q_mid_sem, q_on_sem,
    h1_out, h1_in, h2_out, h2_in, f_out, f_in, m_out, m_in,
):
    me = lax.axis_index("ctx")
    left = (me + N - 1) % N
    right = (me + 1) % N
    loads = [
        pltpu.make_async_copy(src, dst, load_sem.at[i])
        for i, (src, dst) in enumerate(
            ((k_hbm, k_old), (v_hbm, v_old), (q_hbm, q_old), (g_hbm, g_old))
        )
    ]
    for load in loads:
        load.start()
    barrier = pltpu.get_barrier_semaphore()

    def greet(step, carry):
        pl.semaphore_signal(barrier, inc=1, device_id=peer((me + step) % N), device_id_type=MESH)
        return carry

    lax.fori_loop(1, N, greet, 0)

    def find(dest, carry):
        held = 0
        for j in range(PER):
            slot = slots[dest * PER + j]
            held = held + jnp.where((slot >> 4) == me, slot & (PER - 1), 0)
        held_ids[dest] = held
        return carry

    lax.fori_loop(0, N, find, 0)
    loads[0].wait()
    loads[1].wait()

    def pack_kv(dest, carry):
        held = held_ids[dest]
        kv_out[dest, :, :HD] = k_old[held]
        kv_out[dest, :, HD:] = v_old[held]
        return carry

    lax.fori_loop(0, N, pack_kv, 0)
    kv_into[me] = kv_out[me]
    pl.semaphore_wait(barrier, N - 1)

    kvs = Exchange(me, kv_out, kv_into, kv_out_sem, kv_in_sem)
    queries = Exchange(me, q_out, q_into, q_out_sem, q_in_sem, q_mid, q_mid_sem, q_on_sem)
    kvs.push(0, 1)
    for ahead, behind in zip(AHEAD, BEHIND):
        kvs.push(ahead)
        kvs.push(behind)
    kvs.push(NZ // 2)

    loads[2].wait()

    def pack_q(dest, carry):
        q_out[dest] = q_old[held_ids[dest]]
        return carry

    lax.fori_loop(0, N, pack_q, 0)
    q_into[me] = q_out[me]
    queries.push_round(NZ // 2, 0, NX)
    queries.push_round(AHEAD[-1], NX, ROUND)
    queries.push(0, 1)
    for behind, ahead in zip(BEHIND, AHEAD):
        queries.push(behind)
        queries.push(ahead, ROUND if ahead == AHEAD[-1] else 0)

    loads[3].wait()
    for half in range(2):
        for head in range(HEADS):
            cols = slice(half * ROWS + head * TILE, half * ROWS + (head + 1) * TILE)
            part = g_old[half * TILE : (half + 1) * TILE, head * HD : (head + 1) * HD]
            gs[cols] = part
            gt[:, cols] = part.T
    pos = lax.broadcasted_iota(jnp.int32, (1, ROWS), 1) + me * ROWS

    def find_start(doc, carry):
        begin, found = carry
        found = jnp.where(begin <= pos, begin, found)
        return begin + lengths[doc], found

    _, found = lax.fori_loop(0, NDOCS, find_start, (jnp.int32(0), jnp.zeros((1, ROWS), jnp.int32)))
    starts[...] = found - me * ROWS + 2 * ROWS

    kvs.received()

    def unpack_kv(block, carry):
        source = slots[me * PER + block] >> 4
        window[pl.ds(pl.multiple_of(2 * ROWS + block * BLK, BLK), BLK)] = kv_into[source]
        return carry

    lax.fori_loop(0, PER, unpack_kv, 0)

    def hop(level, chunk, out_sem, in_sem):
        return send(
            window.at[pl.ds((2 - level) * ROWS + chunk * SIZE, SIZE)],
            window.at[pl.ds((1 - level) * ROWS + chunk * SIZE, SIZE)],
            out_sem.at[chunk], in_sem.at[chunk], right,
        )

    first = [hop(0, chunk, h1_out, h1_in) for chunk in range(CHUNKS)]
    second = [hop(1, chunk, h2_out, h2_in) for chunk in range(CHUNKS)]
    for copy in first:
        copy.start()
    queries.mid_received()
    queries.pass_on(NZ // 2, 0, NX)
    queries.pass_on(AHEAD[-1], NX, ROUND)
    for copy, onward in zip(first, second):
        copy.wait_recv()
        onward.start()
    kt[:, ROWS:] = window[ROWS:, :HD].T
    vt[:, ROWS:] = window[ROWS:, HD:].T

    def columns(half, head):
        return pl.ds(pl.multiple_of(half * ROWS + head * TILE, TILE), TILE)

    def near_rows(half):
        return slice(ROWS, 2 * ROWS + (half + 1) * TILE)

    def near_dprobs(half):
        rows = near_rows(half)

        def body(head, carry):
            cols = columns(half, head)
            dprobs[rows, cols] = dot_nt(window[rows, HD:], gs[cols])
            return carry

        lax.fori_loop(0, HEADS, body, 0, unroll=True)

    near_dprobs(0)
    near_dprobs(1)
    queries.received()

    def unpack_q(block, carry):
        source = slots[me * PER + block] >> 4
        row = (block // 8) * ROWS + (block % 8) * BLK
        qs[pl.ds(pl.multiple_of(row, BLK), BLK)] = q_into[source, :, :HD]
        qs[pl.ds(pl.multiple_of(row + TILE, BLK), BLK)] = q_into[source, :, HD:]
        return carry

    lax.fori_loop(0, PER, unpack_q, 0)

    def near_forward(half):
        rows = near_rows(half)
        size = rows.stop - rows.start
        pos = lax.broadcasted_iota(jnp.int32, (size, TILE), 0) + ROWS
        query = lax.broadcasted_iota(jnp.int32, (size, TILE), 1) + (2 * ROWS + half * TILE)
        begin = starts[:, half * TILE : (half + 1) * TILE]

        def body(head, carry):
            cols = columns(half, head)
            raw = dot_nt(window[rows, :HD], qs[cols])
            scores = jnp.where((pos >= begin) & (pos <= query), raw * (FACTOR * LOG2E), NEGATIVE)
            peak = jnp.max(scores, axis=0, keepdims=True)
            weights = jnp.exp2(scores - peak)
            probs[rows, cols] = weights
            near_out[:, cols] = dot(vt[:, rows], weights.astype(BF))
            stats[0:1, cols] = peak
            stats[1:2, cols] = jnp.sum(weights, axis=0, keepdims=True)
            return carry

        lax.fori_loop(0, HEADS, body, 0, unroll=True)

    near_forward(0)
    near_forward(1)

    def far_scores(half, row):
        rows = slice(row, row + SIZE)
        pos = lax.broadcasted_iota(jnp.int32, (SIZE, TILE), 0) + row
        begin = starts[:, half * TILE : (half + 1) * TILE]

        def body(head, carry):
            cols = columns(half, head)
            raw = dot_nt(window[rows, :HD], qs[cols])
            probs[rows, cols] = jnp.where(pos >= begin, raw * (FACTOR * LOG2E), NEGATIVE)
            dprobs[rows, cols] = dot_nt(window[rows, HD:], gs[cols])
            return carry

        lax.fori_loop(0, HEADS, body, 0, unroll=True)

    for chunk in range(CHUNKS):
        second[chunk].wait_recv()
        row = chunk * SIZE
        vt[:, row : row + SIZE] = window[row : row + SIZE, HD:].T
        far_scores(0, row)
        if row >= TILE and chunk < CHUNKS - 1:
            far_scores(1, row)

    def far_part(half):
        rows = slice(half * TILE, ROWS)

        def body(head, carry):
            cols = columns(half, head)
            scores = probs[rows, cols]
            near_peak = stats[0:1, cols]
            peak = jnp.maximum(near_peak, jnp.max(scores, axis=0, keepdims=True))
            rescale = jnp.exp2(near_peak - peak)
            weights = jnp.exp2(scores - peak)
            total = stats[1:2, cols] * rescale + jnp.sum(weights, axis=0, keepdims=True)
            inverse = 1.0 / total
            out = near_out[:, cols] * rescale + dot(vt[:, rows], weights.astype(BF))
            out = (out * inverse).astype(BF)
            att[half * TILE : (half + 1) * TILE, pl.ds(pl.multiple_of(head * HD, HD), HD)] = out.T
            delta = jnp.sum(gt[:, cols].astype(F32) * out.astype(F32), axis=0, keepdims=True)
            weights = weights * inverse
            low[rows, cols] = weights.astype(BF)
            dscores[rows, cols] = (weights * (dprobs[rows, cols] - delta)).astype(BF)
            stats[2:3, cols] = rescale * inverse
            stats[3:4, cols] = delta
            return carry

        lax.fori_loop(0, HEADS, body, 0, unroll=True)

    def key_sums(row, cols):
        rows = slice(row, row + SIZE)
        return dot(dscores[rows, cols], qs[cols]) * FACTOR, dot(low[rows, cols], gs[cols])

    back_far = []
    for chunk in range(CHUNKS):
        row = chunk * SIZE
        if row == 0:
            far_part(0)
        if row == TILE:
            far_scores(1, ROWS - SIZE)
            far_part(1)
        cols = slice(0, ROWS if row < TILE else COLS)
        dk, dv = key_sums(row, cols)
        part = slice(row, row + SIZE)
        far_out[part, :HD] = dk.astype(BF)
        far_out[part, HD:] = dv.astype(BF)
        copy = send(far_out.at[pl.ds(row, SIZE)], got_far.at[pl.ds(row, SIZE)], f_out.at[chunk], f_in.at[chunk], left)
        copy.start()
        back_far.append(copy)

    kt[:, :ROWS] = window[:ROWS, :HD].T

    def near_back(half, rows):
        def body(head, carry):
            cols = columns(half, head)
            weights = probs[rows, cols] * stats[2:3, cols]
            low[rows, cols] = weights.astype(BF)
            dscores[rows, cols] = (weights * (dprobs[rows, cols] - stats[3:4, cols])).astype(BF)
            return carry

        lax.fori_loop(0, HEADS, body, 0, unroll=True)

    near_back(0, slice(ROWS, 2 * ROWS))
    near_back(1, slice(ROWS, 2 * ROWS))
    back_mid = []
    for chunk in range(CHUNKS):
        row = chunk * SIZE
        part = slice(row, row + SIZE)
        dk, dv = key_sums(ROWS + row, slice(0, COLS))
        back_far[chunk].wait_recv()
        mid_out[part, :HD] = (dk + got_far[part, :HD].astype(F32)).astype(BF)
        mid_out[part, HD:] = (dv + got_far[part, HD:].astype(F32)).astype(BF)
        copy = send(mid_out.at[pl.ds(row, SIZE)], got_hbm.at[pl.ds(row, SIZE)], m_out.at[chunk], m_in.at[chunk], left)
        copy.start()
        back_mid.append(copy)

    near_back(0, slice(2 * ROWS, 2 * ROWS + TILE))
    near_back(1, slice(2 * ROWS, 3 * ROWS))
    for chunk in range(CHUNKS):
        row = chunk * SIZE
        part = slice(row, row + SIZE)
        cols = slice(0 if row < TILE else ROWS, COLS)
        dk, dv = key_sums(2 * ROWS + row, cols)
        own[part, :HD] = dk
        own[part, HD:] = dv

    def query_grad(half):
        rows = slice(half * TILE, 2 * ROWS + (half + 1) * TILE)

        def body(head, carry):
            cols = columns(half, head)
            grad = dot(kt[:, rows], dscores[rows, cols]) * FACTOR
            dq[half * TILE : (half + 1) * TILE, pl.ds(pl.multiple_of(head * HD, HD), HD)] = grad.T
            return carry

        lax.fori_loop(0, HEADS, body, 0, unroll=True)

    query_grad(0)
    query_grad(1)
    stores = [
        pltpu.make_async_copy(src, dst, store_sem.at[i])
        for i, (src, dst) in enumerate(((att, att_hbm), (dq, dq_hbm), (own, own_hbm)))
    ]
    for store in stores:
        store.start()
    kvs.sent()
    queries.sent()
    queries.passed_on()
    for copy in first + second + back_far + back_mid:
        copy.wait_send()
    for store in stores:
        store.wait()
    for copy in back_mid:
        copy.wait_recv()


def finish_kernel(
    att_hbm, dq_hbm, own_hbm, got_hbm, att_ref, dq_ref, dk_ref, dv_ref,
    att, dq, own, got, dk, dv, load_sem, store_sem,
):
    halves = [pl.ds(half * TILE, TILE) for half in range(2)]
    loads = []
    for half, rows in enumerate(halves):
        loads.append([
            pltpu.make_async_copy(src.at[rows], dst.at[rows], load_sem.at[half, i])
            for i, (src, dst) in enumerate(
                ((got_hbm, got), (own_hbm, own), (att_hbm, att), (dq_hbm, dq))
            )
        ])
        for load in loads[half]:
            load.start()
    stores = []

    def store(half, i, src, dst):
        copy = pltpu.make_async_copy(src.at[halves[half]], dst.at[halves[half]], store_sem.at[half, i])
        copy.start()
        stores.append(copy)

    for half, rows in enumerate(halves):
        loads[half][0].wait()
        loads[half][1].wait()
        dk[rows] = own[rows, :HD] + got[rows, :HD].astype(F32)
        store(half, 0, dk, dk_ref)
        dv[rows] = own[rows, HD:] + got[rows, HD:].astype(F32)
        store(half, 1, dv, dv_ref)
        loads[half][2].wait()
        store(half, 2, att, att_ref)
        loads[half][3].wait()
        store(half, 3, dq, dq_ref)
    for copy in stores:
        copy.wait()


def specs(space, count):
    return [pl.BlockSpec(memory_space=space)] * count


def shape(*dims, dtype=BF):
    return jax.ShapeDtypeStruct(dims, dtype)


def on_device(queries, keys, values, cotangent, doc_lengths, old_slots):
    dma = pltpu.SemaphoreType.DMA
    bf = lambda *dims: pltpu.VMEM(dims, BF)
    f32 = lambda *dims: pltpu.VMEM(dims, F32)
    out_shape = [
        shape(ROWS, 2 * HD),
        shape(ROWS, 2 * HD, dtype=F32),
    ]
    results = pl.pallas_call(
        main_kernel,
        out_shape=out_shape + [shape(ROWS, 2 * HD, dtype=F32), shape(ROWS, 2 * HD)],
        in_specs=specs(pltpu.SMEM, 2) + specs(pltpu.HBM, 4),
        out_specs=specs(pltpu.HBM, 4),
        scratch_shapes=[bf(PER, BLK, 2 * HD), bf(PER, BLK, HD), bf(PER, BLK, HD), bf(ROWS, 2 * HD)]
        + [pltpu.SMEM((N,), jnp.int32)]
        + [bf(N, BLK, 2 * HD)] * 4
        + [bf(NX + ROUND, BLK, 2 * HD)]
        + [bf(WIN, 2 * HD), bf(HD, WIN), bf(HD, WIN), bf(COLS, HD), bf(COLS, HD), bf(HD, COLS)]
        + [pltpu.VMEM((1, ROWS), jnp.int32)]
        + [f32(WIN, COLS), f32(WIN, COLS), bf(WIN, COLS), bf(WIN, COLS), f32(HD, COLS), f32(8, COLS)]
        + [bf(ROWS, 2 * HD)] * 4
        + [f32(ROWS, 2 * HD)] * 2
        + [dma((4,)), dma((3,))]
        + [dma(())] * 6
        + [dma((CHUNKS,))] * 8,
        compiler_params=pltpu.CompilerParams(
            collective_id=0, has_side_effects=True, vmem_limit_bytes=56 << 20
        ),
        name="exchange_and_attend",
    )(
        old_slots, doc_lengths,
        queries.reshape(PER, BLK, 2 * HD),
        keys.reshape(PER, BLK, HD),
        values.reshape(PER, BLK, HD),
        cotangent,
    )
    return pl.pallas_call(
        finish_kernel,
        out_shape=out_shape + [shape(ROWS, HD, dtype=F32)] * 2,
        in_specs=specs(pltpu.HBM, 4),
        out_specs=specs(pltpu.HBM, 4),
        scratch_shapes=[bf(ROWS, 2 * HD), f32(ROWS, 2 * HD), f32(ROWS, 2 * HD), bf(ROWS, 2 * HD)]
        + [f32(ROWS, HD)] * 2
        + [dma((2, 4))] * 2,
        compiler_params=pltpu.CompilerParams(vmem_limit_bytes=56 << 20),
        name="finish",
    )(*results)


def solution(mesh):
    rows = P(("dp", "ctx"), None)
    return jax.shard_map(
        on_device,
        mesh=mesh,
        in_specs=(rows, rows, rows, rows, P("dp"), P("dp")),
        out_specs=(rows, rows, rows, rows),
        check_vma=False,
    )
```

```python
import jax
import jax.numpy as jnp
from jax import lax
from jax.experimental import pallas as pl
from jax.experimental.pallas import tpu as pltpu
from jax.sharding import PartitionSpec as P

N = 32
NZ = 8
NX = 4
BLK = 32
PER = 16
ROWS = 512
HD = 128
HEADS = 2
WIN = 3 * ROWS
TILE = 256
COLS = HEADS * ROWS
NDOCS = 64
CHUNKS = 4
SIZE = ROWS // CHUNKS
NEGATIVE = -1e30
LOG2E = 1.4426950408889634
FACTOR = HD**-0.5
MESH = pl.DeviceIdType.MESH
BF = jnp.bfloat16
F32 = jnp.float32
BEHIND = (7, 6, 5)
AHEAD = (1, 2, 3)
ROUND = 1


def peer(index):
    return (lax.axis_index("dp"), index)


def send(src, dst, send_sem, recv_sem, index):
    return pltpu.make_async_remote_copy(
        src, dst, send_sem, recv_sem, device_id=peer(index), device_id_type=MESH
    )


def near_first(step):
    return jnp.where(step < 2, step, 5 - step)


def dot_nt(left, right):
    return lax.dot_general(left, right, (((1,), (1,)), ((), ())), preferred_element_type=F32)


def dot(left, right):
    return jnp.dot(left, right, preferred_element_type=F32)


class Exchange:
    def __init__(self, me, out, into, out_sem, in_sem, mid=None, mid_sem=None, onward_sem=None):
        self.me = me
        self.out, self.into, self.mid = out, into, mid
        self.out_sem, self.in_sem = out_sem, in_sem
        self.mid_sem, self.onward_sem = mid_sem, onward_sem

    def at(self, dx, dz):
        x = (self.me // NZ + dx) % NX
        z = (self.me % NZ + dz) % NZ
        return x * NZ + z

    def push(self, dz, first=0):
        def body(step, carry):
            dest = self.at(near_first(step), dz)
            send(self.out.at[dest], self.into.at[self.me], self.out_sem, self.in_sem, dest).start()
            return carry

        lax.fori_loop(first, NX, body, 0)

    def push_round(self, dz, spot, count):
        def body(step, carry):
            dx = near_first(step)
            dest = self.at(dx, dz)
            way = self.at(dx, NZ - 2)
            send(
                self.out.at[dest], self.mid.at[spot + step], self.out_sem, self.mid_sem, way
            ).start()
            return carry

        lax.fori_loop(0, count, body, 0)

    def mid_received(self):
        pltpu.make_async_copy(self.mid, self.mid, self.mid_sem).wait()

    def pass_on(self, dz, spot, count):
        dest = self.at(0, dz + 2)

        def body(step, carry):
            source = self.at(NX - near_first(step), 2)
            send(
                self.mid.at[spot + step], self.into.at[source], self.onward_sem, self.in_sem, dest
            ).start()
            return carry

        lax.fori_loop(0, count, body, 0)

    def received(self):
        part = self.into.at[pl.ds(0, N - 1)]
        pltpu.make_async_copy(part, part, self.in_sem).wait()

    def sent(self):
        part = self.out.at[pl.ds(0, N - 1)]
        pltpu.make_async_copy(part, part, self.out_sem).wait()

    def passed_on(self):
        pltpu.make_async_copy(self.mid, self.mid, self.onward_sem).wait()


def main_kernel(
    slots, lengths, q_hbm, k_hbm, v_hbm, g_hbm,
    att_hbm, dq_hbm, own_hbm, got_hbm,
    q_old, k_old, v_old, g_old, held_ids,
    kv_out, kv_into, q_out, q_into, q_mid,
    window, kt, vt, qs, gs, gt, starts,
    probs, dprobs, low, dscores, near_out, stats,
    far_out, got_far, mid_out, att, dq, own,
    load_sem, store_sem, kv_out_sem, kv_in_sem, q_out_sem, q_in_sem, q_mid_sem, q_on_sem,
    h1_out, h1_in, h2_out, h2_in, f_out, f_in, m_out, m_in,
):
    me = lax.axis_index("ctx")
    left = (me + N - 1) % N
    right = (me + 1) % N
    loads = [
        pltpu.make_async_copy(src, dst, load_sem.at[i])
        for i, (src, dst) in enumerate(
            ((k_hbm, k_old), (v_hbm, v_old), (q_hbm, q_old), (g_hbm, g_old))
        )
    ]
    for load in loads:
        load.start()
    barrier = pltpu.get_barrier_semaphore()

    def greet(step, carry):
        pl.semaphore_signal(barrier, inc=1, device_id=peer((me + step) % N), device_id_type=MESH)
        return carry

    lax.fori_loop(1, N, greet, 0)

    def find(dest, carry):
        held = 0
        for j in range(PER):
            slot = slots[dest * PER + j]
            held = held + jnp.where((slot >> 4) == me, slot & (PER - 1), 0)
        held_ids[dest] = held
        return carry

    lax.fori_loop(0, N, find, 0)
    loads[0].wait()
    loads[1].wait()

    def pack_kv(dest, carry):
        held = held_ids[dest]
        kv_out[dest, :, :HD] = k_old[held]
        kv_out[dest, :, HD:] = v_old[held]
        return carry

    lax.fori_loop(0, N, pack_kv, 0)
    kv_into[me] = kv_out[me]
    pl.semaphore_wait(barrier, N - 1)

    kvs = Exchange(me, kv_out, kv_into, kv_out_sem, kv_in_sem)
    queries = Exchange(me, q_out, q_into, q_out_sem, q_in_sem, q_mid, q_mid_sem, q_on_sem)
    kvs.push(0, 1)
    for ahead, behind in zip(AHEAD, BEHIND):
        kvs.push(ahead)
        kvs.push(behind)
    kvs.push(NZ // 2)

    loads[2].wait()

    def pack_q(dest, carry):
        q_out[dest] = q_old[held_ids[dest]]
        return carry

    lax.fori_loop(0, N, pack_q, 0)
    q_into[me] = q_out[me]
    queries.push_round(NZ // 2, 0, NX)
    queries.push_round(AHEAD[-1], NX, ROUND)
    queries.push(0, 1)
    for behind, ahead in zip(BEHIND, AHEAD):
        queries.push(behind)
        queries.push(ahead, ROUND if ahead == AHEAD[-1] else 0)

    loads[3].wait()
    for half in range(2):
        for head in range(HEADS):
            cols = slice(half * ROWS + head * TILE, half * ROWS + (head + 1) * TILE)
            part = g_old[half * TILE : (half + 1) * TILE, head * HD : (head + 1) * HD]
            gs[cols] = part
            gt[:, cols] = part.T
    pos = lax.broadcasted_iota(jnp.int32, (1, ROWS), 1) + me * ROWS

    def find_start(doc, carry):
        begin, found = carry
        found = jnp.where(begin <= pos, begin, found)
        return begin + lengths[doc], found

    _, found = lax.fori_loop(0, NDOCS, find_start, (jnp.int32(0), jnp.zeros((1, ROWS), jnp.int32)))
    starts[...] = found - me * ROWS + 2 * ROWS

    kvs.received()

    def unpack_kv(block, carry):
        source = slots[me * PER + block] >> 4
        window[pl.ds(pl.multiple_of(2 * ROWS + block * BLK, BLK), BLK)] = kv_into[source]
        return carry


    def hop(level, chunk, out_sem, in_sem):
        return send(
            window.at[pl.ds((2 - level) * ROWS + chunk * SIZE, SIZE)],
            window.at[pl.ds((1 - level) * ROWS + chunk * SIZE, SIZE)],
            out_sem.at[chunk], in_sem.at[chunk], right,
        )

    first = [hop(0, chunk, h1_out, h1_in) for chunk in range(CHUNKS)]
    second = [hop(1, chunk, h2_out, h2_in) for chunk in range(CHUNKS)]
    blocks = PER // CHUNKS
    for chunk, copy in enumerate(first):
        lax.fori_loop(chunk * blocks, (chunk + 1) * blocks, unpack_kv, 0)
        copy.start()
    queries.mid_received()
    queries.pass_on(NZ // 2, 0, NX)
    queries.pass_on(AHEAD[-1], NX, ROUND)
    for copy, onward in zip(first, second):
        copy.wait_recv()
        onward.start()
    kt[:, ROWS:] = window[ROWS:, :HD].T
    vt[:, ROWS:] = window[ROWS:, HD:].T

    def columns(half, head):
        return pl.ds(pl.multiple_of(half * ROWS + head * TILE, TILE), TILE)

    def near_rows(half):
        return slice(ROWS, 2 * ROWS + (half + 1) * TILE)

    def near_dprobs(half):
        rows = near_rows(half)

        def body(head, carry):
            cols = columns(half, head)
            dprobs[rows, cols] = dot_nt(window[rows, HD:], gs[cols])
            return carry

        lax.fori_loop(0, HEADS, body, 0, unroll=True)

    near_dprobs(0)
    near_dprobs(1)
    queries.received()

    def unpack_q(block, carry):
        source = slots[me * PER + block] >> 4
        row = (block // 8) * ROWS + (block % 8) * BLK
        qs[pl.ds(pl.multiple_of(row, BLK), BLK)] = q_into[source, :, :HD]
        qs[pl.ds(pl.multiple_of(row + TILE, BLK), BLK)] = q_into[source, :, HD:]
        return carry

    lax.fori_loop(0, PER, unpack_q, 0)

    def near_forward(half):
        rows = near_rows(half)
        size = rows.stop - rows.start
        pos = lax.broadcasted_iota(jnp.int32, (size, TILE), 0) + ROWS
        query = lax.broadcasted_iota(jnp.int32, (size, TILE), 1) + (2 * ROWS + half * TILE)
        begin = starts[:, half * TILE : (half + 1) * TILE]

        def body(head, carry):
            cols = columns(half, head)
            raw = dot_nt(window[rows, :HD], qs[cols])
            scores = jnp.where((pos >= begin) & (pos <= query), raw * (FACTOR * LOG2E), NEGATIVE)
            peak = jnp.max(scores, axis=0, keepdims=True)
            weights = jnp.exp2(scores - peak)
            probs[rows, cols] = weights
            near_out[:, cols] = dot(vt[:, rows], weights.astype(BF))
            stats[0:1, cols] = peak
            stats[1:2, cols] = jnp.sum(weights, axis=0, keepdims=True)
            return carry

        lax.fori_loop(0, HEADS, body, 0, unroll=True)

    near_forward(0)
    near_forward(1)

    def far_scores(half, row):
        rows = slice(row, row + SIZE)
        pos = lax.broadcasted_iota(jnp.int32, (SIZE, TILE), 0) + row
        begin = starts[:, half * TILE : (half + 1) * TILE]

        def body(head, carry):
            cols = columns(half, head)
            raw = dot_nt(window[rows, :HD], qs[cols])
            probs[rows, cols] = jnp.where(pos >= begin, raw * (FACTOR * LOG2E), NEGATIVE)
            dprobs[rows, cols] = dot_nt(window[rows, HD:], gs[cols])
            return carry

        lax.fori_loop(0, HEADS, body, 0, unroll=True)

    for chunk in range(CHUNKS):
        second[chunk].wait_recv()
        row = chunk * SIZE
        vt[:, row : row + SIZE] = window[row : row + SIZE, HD:].T
        far_scores(0, row)
        if row >= TILE and chunk < CHUNKS - 1:
            far_scores(1, row)

    def far_part(half):
        rows = slice(half * TILE, ROWS)

        def body(head, carry):
            cols = columns(half, head)
            scores = probs[rows, cols]
            near_peak = stats[0:1, cols]
            peak = jnp.maximum(near_peak, jnp.max(scores, axis=0, keepdims=True))
            rescale = jnp.exp2(near_peak - peak)
            weights = jnp.exp2(scores - peak)
            total = stats[1:2, cols] * rescale + jnp.sum(weights, axis=0, keepdims=True)
            inverse = 1.0 / total
            out = near_out[:, cols] * rescale + dot(vt[:, rows], weights.astype(BF))
            out = (out * inverse).astype(BF)
            att[half * TILE : (half + 1) * TILE, pl.ds(pl.multiple_of(head * HD, HD), HD)] = out.T
            delta = jnp.sum(gt[:, cols].astype(F32) * out.astype(F32), axis=0, keepdims=True)
            weights = weights * inverse
            low[rows, cols] = weights.astype(BF)
            dscores[rows, cols] = (weights * (dprobs[rows, cols] - delta)).astype(BF)
            stats[2:3, cols] = rescale * inverse
            stats[3:4, cols] = delta
            return carry

        lax.fori_loop(0, HEADS, body, 0, unroll=True)

    def key_sums(row, cols):
        rows = slice(row, row + SIZE)
        return dot(dscores[rows, cols], qs[cols]) * FACTOR, dot(low[rows, cols], gs[cols])

    back_far = []
    for chunk in range(CHUNKS):
        row = chunk * SIZE
        if row == 0:
            far_part(0)
        if row == TILE:
            far_scores(1, ROWS - SIZE)
            far_part(1)
        cols = slice(0, ROWS if row < TILE else COLS)
        dk, dv = key_sums(row, cols)
        part = slice(row, row + SIZE)
        far_out[part, :HD] = dk.astype(BF)
        far_out[part, HD:] = dv.astype(BF)
        copy = send(far_out.at[pl.ds(row, SIZE)], got_far.at[pl.ds(row, SIZE)], f_out.at[chunk], f_in.at[chunk], left)
        copy.start()
        back_far.append(copy)

    kt[:, :ROWS] = window[:ROWS, :HD].T

    def near_back(half, rows):
        def body(head, carry):
            cols = columns(half, head)
            weights = probs[rows, cols] * stats[2:3, cols]
            low[rows, cols] = weights.astype(BF)
            dscores[rows, cols] = (weights * (dprobs[rows, cols] - stats[3:4, cols])).astype(BF)
            return carry

        lax.fori_loop(0, HEADS, body, 0, unroll=True)

    near_back(0, slice(ROWS, 2 * ROWS))
    near_back(1, slice(ROWS, 2 * ROWS))
    back_mid = []
    for chunk in range(CHUNKS):
        row = chunk * SIZE
        part = slice(row, row + SIZE)
        dk, dv = key_sums(ROWS + row, slice(0, COLS))
        back_far[chunk].wait_recv()
        mid_out[part, :HD] = (dk + got_far[part, :HD].astype(F32)).astype(BF)
        mid_out[part, HD:] = (dv + got_far[part, HD:].astype(F32)).astype(BF)
        copy = send(mid_out.at[pl.ds(row, SIZE)], got_hbm.at[pl.ds(row, SIZE)], m_out.at[chunk], m_in.at[chunk], left)
        copy.start()
        back_mid.append(copy)

    near_back(0, slice(2 * ROWS, 2 * ROWS + TILE))
    near_back(1, slice(2 * ROWS, 3 * ROWS))
    for chunk in range(CHUNKS):
        row = chunk * SIZE
        part = slice(row, row + SIZE)
        cols = slice(0 if row < TILE else ROWS, COLS)
        dk, dv = key_sums(2 * ROWS + row, cols)
        own[part, :HD] = dk
        own[part, HD:] = dv

    def query_grad(half):
        rows = slice(half * TILE, 2 * ROWS + (half + 1) * TILE)

        def body(head, carry):
            cols = columns(half, head)
            grad = dot(kt[:, rows], dscores[rows, cols]) * FACTOR
            dq[half * TILE : (half + 1) * TILE, pl.ds(pl.multiple_of(head * HD, HD), HD)] = grad.T
            return carry

        lax.fori_loop(0, HEADS, body, 0, unroll=True)

    query_grad(0)
    query_grad(1)
    stores = [
        pltpu.make_async_copy(src, dst, store_sem.at[i])
        for i, (src, dst) in enumerate(((att, att_hbm), (dq, dq_hbm), (own, own_hbm)))
    ]
    for store in stores:
        store.start()
    kvs.sent()
    queries.sent()
    queries.passed_on()
    for copy in first + second + back_far + back_mid:
        copy.wait_send()
    for store in stores:
        store.wait()
    for copy in back_mid:
        copy.wait_recv()


def finish_kernel(
    att_hbm, dq_hbm, own_hbm, got_hbm, att_ref, dq_ref, dk_ref, dv_ref,
    att, dq, own, got, dk, dv, load_sem, store_sem,
):
    halves = [pl.ds(half * TILE, TILE) for half in range(2)]
    loads = []
    for half, rows in enumerate(halves):
        loads.append([
            pltpu.make_async_copy(src.at[rows], dst.at[rows], load_sem.at[half, i])
            for i, (src, dst) in enumerate(
                ((got_hbm, got), (own_hbm, own), (att_hbm, att), (dq_hbm, dq))
            )
        ])
        for load in loads[half]:
            load.start()
    stores = []

    def store(half, i, src, dst):
        copy = pltpu.make_async_copy(src.at[halves[half]], dst.at[halves[half]], store_sem.at[half, i])
        copy.start()
        stores.append(copy)

    for half, rows in enumerate(halves):
        loads[half][0].wait()
        loads[half][1].wait()
        dk[rows] = own[rows, :HD] + got[rows, :HD].astype(F32)
        store(half, 0, dk, dk_ref)
        dv[rows] = own[rows, HD:] + got[rows, HD:].astype(F32)
        store(half, 1, dv, dv_ref)
        loads[half][2].wait()
        store(half, 2, att, att_ref)
        loads[half][3].wait()
        store(half, 3, dq, dq_ref)
    for copy in stores:
        copy.wait()


def specs(space, count):
    return [pl.BlockSpec(memory_space=space)] * count


def shape(*dims, dtype=BF):
    return jax.ShapeDtypeStruct(dims, dtype)


def on_device(queries, keys, values, cotangent, doc_lengths, old_slots):
    dma = pltpu.SemaphoreType.DMA
    bf = lambda *dims: pltpu.VMEM(dims, BF)
    f32 = lambda *dims: pltpu.VMEM(dims, F32)
    out_shape = [
        shape(ROWS, 2 * HD),
        shape(ROWS, 2 * HD, dtype=F32),
    ]
    results = pl.pallas_call(
        main_kernel,
        out_shape=out_shape + [shape(ROWS, 2 * HD, dtype=F32), shape(ROWS, 2 * HD)],
        in_specs=specs(pltpu.SMEM, 2) + specs(pltpu.HBM, 4),
        out_specs=specs(pltpu.HBM, 4),
        scratch_shapes=[bf(PER, BLK, 2 * HD), bf(PER, BLK, HD), bf(PER, BLK, HD), bf(ROWS, 2 * HD)]
        + [pltpu.SMEM((N,), jnp.int32)]
        + [bf(N, BLK, 2 * HD)] * 4
        + [bf(NX + ROUND, BLK, 2 * HD)]
        + [bf(WIN, 2 * HD), bf(HD, WIN), bf(HD, WIN), bf(COLS, HD), bf(COLS, HD), bf(HD, COLS)]
        + [pltpu.VMEM((1, ROWS), jnp.int32)]
        + [f32(WIN, COLS), f32(WIN, COLS), bf(WIN, COLS), bf(WIN, COLS), f32(HD, COLS), f32(8, COLS)]
        + [bf(ROWS, 2 * HD)] * 4
        + [f32(ROWS, 2 * HD)] * 2
        + [dma((4,)), dma((3,))]
        + [dma(())] * 6
        + [dma((CHUNKS,))] * 8,
        compiler_params=pltpu.CompilerParams(
            collective_id=0, has_side_effects=True, vmem_limit_bytes=56 << 20
        ),
        name="exchange_and_attend",
    )(
        old_slots, doc_lengths,
        queries.reshape(PER, BLK, 2 * HD),
        keys.reshape(PER, BLK, HD),
        values.reshape(PER, BLK, HD),
        cotangent,
    )
    return pl.pallas_call(
        finish_kernel,
        out_shape=out_shape + [shape(ROWS, HD, dtype=F32)] * 2,
        in_specs=specs(pltpu.HBM, 4),
        out_specs=specs(pltpu.HBM, 4),
        scratch_shapes=[bf(ROWS, 2 * HD), f32(ROWS, 2 * HD), f32(ROWS, 2 * HD), bf(ROWS, 2 * HD)]
        + [f32(ROWS, HD)] * 2
        + [dma((2, 4))] * 2,
        compiler_params=pltpu.CompilerParams(vmem_limit_bytes=56 << 20),
        name="finish",
    )(*results)


def solution(mesh):
    rows = P(("dp", "ctx"), None)
    return jax.shard_map(
        on_device,
        mesh=mesh,
        in_specs=(rows, rows, rows, rows, P("dp"), P("dp")),
        out_specs=(rows, rows, rows, rows),
        check_vma=False,
    )
```
